32 devices in a mesh: groups: 2 (over y), slab: 4 (over z), side: 4 (over x, core).
Axes of the slice: x: 2, y: 2, z: 4, core: 2. Of those that a mesh axis runs over, the one named last changes fastest.
Arguments:
- populations: float32 [19, 32, 256, 128], P(None, ('groups', 'slab'), 'side'), parts along dimension 1, may hold values from 0.5 to 1.5
- solid_mask: int32 [32, 256, 128], P(('groups', 'slab'), 'side'), parts along dimension 0, may hold values 0 or 1
- point_cell: int32 [65536], P(('groups', 'slab', 'side')), parts along dimension 0, may hold values from 0 to 32767
- point_owner: int32 [65536, 1], P(('groups', 'slab', 'side')), parts along dimension 0, may hold values from 0 to 15; in each aligned block of 2048 rows (0 to 2047, 2048 to 4095, ...) at most 256 rows name the same one
- point_block: int32 [65536], P(('groups', 'slab', 'side')), parts along dimension 0, may hold values from 0 to 7
- point_coords: float32 [3, 65536], P(None, ('groups', 'slab', 'side')), parts along dimension 1, may hold values from 0 to 1
- point_normal: float32 [3, 65536], P(None, ('groups', 'slab', 'side')), parts along dimension 1, may hold values from -1 to 1
- node_coords: float32 [3, 32768], P(None, ('groups', 'slab', 'side')), parts along dimension 1, may hold values from 0 to 1
- struct_prev: float32 [3, 32768], P(None, ('groups', 'slab', 'side')), parts along dimension 1, may hold values from -6 to 6
- compliance: float32 [32768], P(('groups', 'slab', 'side')), parts along dimension 0, may hold values from 0.5 to 2
- elem_nodes: int32 [4, 32768], P(None, ('groups', 'slab', 'side')), parts along dimension 1, may hold values from 0 to 1023
- elem_stiff: float32 [12, 12, 32768], P(None, None, ('groups', 'slab', 'side')), parts along dimension 2, may hold values from -1.75 to 1.75
- iterate: float32 [3, 65536], P(None, ('groups', 'slab', 'side')), parts along dimension 1
- resid_prev: float32 [3, 65536], P(None, ('groups', 'slab', 'side')), parts along dimension 1, may hold values from -6 to 6
- image_prev: float32 [3, 65536], P(None, ('groups', 'slab', 'side')), parts along dimension 1, may hold values from -6 to 6
- resid_history: float32 [4, 3, 65536], P(None, None, ('groups', 'slab', 'side')), parts along dimension 2
- image_history: float32 [4, 3, 65536], P(None, None, ('groups', 'slab', 'side')), parts along dimension 2, may hold values from -6 to 6
Outputs:
- populations_next: float32 [19, 32, 256, 128], P(None, ('groups', 'slab'), 'side'), parts along dimension 1
- struct_disp: float32 [3, 32768], P(None, ('groups', 'slab', 'side')), parts along dimension 1
- iterate_next: float32 [3, 65536], P(None, ('groups', 'slab', 'side')), parts along dimension 1
The draws below stay inside these ranges and needn't reach their ends.
There are 2 independent parts, one for each index of `groups`. The reference program is written for one: setup_inputs(seed, part) draws one part's arguments, and reference() takes and returns one part's arrays. A program takes and returns all parts, laid end to end along the dimension named above; each array names one. Nothing has to cross between parts.
Inputs may be any that keep to these rules, and one draw needn't show every extreme that they name: `point_cell`: cells are numbered within the point's own device's block of 4 x 64 x 128 cells, y fastest. `point_owner`: devices numbered slab * 4 + side; among one device's 2048 points at most 256 name the same owner, and in every draw some owner is named by exactly 256 of them. `point_block`: block number within the owner's 8 blocks. `elem_nodes`: node numbers within the device that holds the element.
All inputs are finite; a program needn't handle non-finite values. No bound on the sum of `solid_mask` on one device may be relied on, other than what follows from the above.
Results may differ from the reference program's by a relative error of at most 0.0003.
Values sent between devices are 32-bit elements; how exact they have to be, the bound alone decides.
A program may use at most 64 MiB of HBM per device.

```python
import math
import jax
import jax.numpy as jnp
import numpy as np
from jax import lax

LZ_DEV = 4
LX_DEV = 64
NY = 128
IP_DEV = 2048
NODE_DEV = 1024
RBF_BLOCK = 128
HIST = 4
CAP = 256
SB_DEV = 8
NZ = 16
NX = 256
NPTS = 32768
NODES = 16384
NELEM = 16384
N_SLAB = 4
N_SIDE = 4


def history_base(key, power):
    base = jax.random.normal(key, (HIST, 3, NPTS), jnp.float32)
    ramp = 1.0 + 2.0 * jnp.arange(NPTS, dtype=jnp.float32) / NPTS
    return base * (ramp ** power)[None, None, :]


def draw_resid_history(key, part):
    power = 1.0
    base = history_base(key, power)
    return base


def draw_iterate(key, part):
    power = 1.0
    base = history_base(key, power)
    key = jax.random.fold_in(key, 23)
    order = jnp.arange(HIST, dtype=jnp.float32)
    parity = 1.0 - 2.0 * (jnp.arange(HIST) % 2).astype(jnp.float32)
    factors = parity * (0.9 - 0.6 * order / HIST)
    noise = 0.5 * jax.random.normal(key, (3, NPTS), jnp.float32)
    return jnp.sum(factors[:, None, None] * base, axis=0) + noise


def plant(entries, own_key, smallest, top_value):
    dims = entries.shape
    spot = [jax.random.randint(jax.random.fold_in(own_key, axis), (), 0, dims[axis]) for axis in range(len(dims))]
    entries = entries.at[tuple(spot)].set(smallest)
    longest = dims.index(max(dims))
    spot[longest] = (spot[longest] + 1) % dims[longest]
    return entries.at[tuple(spot)].set(top_value)


def steps_of(key, shape, cuts, least, largest):
    def one(position, blocks):
        heights = jax.random.uniform(jax.random.fold_in(jax.random.fold_in(key, 6), position), (blocks,), jnp.float32, least / len(cuts), largest / len(cuts))
        return jnp.repeat(jnp.exp(heights), shape[position] // blocks).reshape((-1,) + (1,) * (len(shape) - position - 1))

    factor_of = one(*cuts[0])
    for cut in cuts[1:]:
        factor_of = factor_of * one(*cut)
    return factor_of


def routed_block(own_key, own, number, rows, amount, top, limit, slope):
    sequence = jax.random.permutation(own_key, amount)
    crowded, usual = shares(amount, rows * top, limit, slope, True), shares(amount, rows * top, limit, slope, False)
    places = jnp.arange(amount)

    def named(tallies, rotation):
        used = int((tallies > 0).sum())
        fixed = max(1, used // 4)
        shifted = fixed + (places - fixed + rotation * (used - fixed)) % max(1, amount - fixed)
        return jnp.zeros((amount,), jnp.int32).at[sequence[jnp.where(places < fixed, places, shifted)]].set(jnp.asarray(tallies, jnp.int32))

    tallies = jnp.where(number % 4 == 0, named(crowded, number // 4), named(usual, number - number // 4 - 1))
    mixed = jax.random.permutation(jax.random.fold_in(own, 3), amount)
    donor, sink = mixed[0:amount // 2 * 2:2], mixed[1:amount // 2 * 2:2]
    margin = jnp.minimum(tallies[donor] - 1, limit - tallies[sink]) // 2
    margin = jnp.where((donor == sequence[0]) | (sink == sequence[0]) | (tallies[sink] == 0), 0, jnp.maximum(margin, 0))
    shifted = jax.random.randint(jax.random.fold_in(own, 4), (amount // 2,), 0, 1 << 20) % (margin + 1)
    tallies = tallies.at[donor].add(-shifted).at[sink].add(shifted)
    items = jnp.searchsorted(jnp.cumsum(tallies), jnp.arange(rows * top), side="right").astype(jnp.int32)
    table = items.reshape(top, rows).T
    table = table[jax.random.permutation(jax.random.fold_in(own, 1), rows)]
    rotation = jax.random.randint(jax.random.fold_in(own, 2), (rows, 1), 0, top)
    return jnp.take_along_axis(table, (jnp.arange(top)[None, :] + rotation) % top, axis=1)


def shares(count, total, bound, skew, full):
    weights = [(1 << 20) // math.isqrt(grade ** skew) + 1 for grade in range(1, count + 1)]
    largest = bound if full else min(bound, max(-(-total // count), total * weights[0] // sum(weights)))
    least = 1 if total - largest >= count - 1 else 0
    counts, surplus = [largest] + [least] * (count - 1), total - largest - least * (count - 1)
    while surplus > 0:
        candidates = [i for i in range(1, count) if counts[i] < largest] or [i for i in range(1, count) if counts[i] < bound]
        pool, left = sum([weights[i] for i in candidates]), surplus
        for i in candidates:
            more = min(bound - counts[i], max(1, left * weights[i] // pool), surplus)
            counts[i] = counts[i] + more
            surplus = surplus - more
    return np.array(counts)


def bell_draw(own_key, dims, scale, bound, pieces=(), kind=jnp.bfloat16):
    values = scale * jax.random.normal(own_key, dims, jnp.float32)
    if pieces:
        values = values * steps_of(own_key, dims, pieces, -0.22, 0.18)
    return jnp.clip(values, -bound, bound).astype(kind)


def setup_inputs(seed: int = 0, part: int = 0) -> dict:
    key_of = jax.random.split(jax.random.key(seed), 18)
    part_splits = jax.random.split(jax.random.fold_in(key_of[17], part), 18)
    populations = jnp.clip(0.5 + 1.0 * jax.random.uniform(part_splits[0], (19, NZ, NX, NY), jnp.float32) ** steps_of(part_splits[0], (19, NZ, NX, NY), ((1, 4), (2, 4)), -0.2, 0.2), 0.5, 1.5)
    solid_mask = plant((jax.random.randint(part_splits[1], (NZ, NX, NY), 0, 8) < 1).astype(jnp.int32), jax.random.fold_in(part_splits[1], 1), 0, 1)
    point_cell = plant(jax.random.randint(part_splits[2], (NPTS,), 0, LZ_DEV * LX_DEV * NY), jax.random.fold_in(part_splits[2], 1), 0, (LZ_DEV * LX_DEV * NY) - 1).astype(jnp.int32)
    point_owner_keys = jax.random.split(jax.random.fold_in(part_splits[3], 1), NPTS // IP_DEV)
    point_owner_turns = jax.random.permutation(jax.random.fold_in(part_splits[3], 3), NPTS // IP_DEV)
    point_owner = jax.vmap(lambda own, number: routed_block(jax.random.fold_in(part_splits[3], 2), own, number, IP_DEV, N_SLAB * N_SIDE, 1, CAP, 2))(point_owner_keys, point_owner_turns).reshape((NPTS, 1))
    point_block = plant(jax.random.randint(part_splits[4], (NPTS,), 0, SB_DEV), jax.random.fold_in(part_splits[4], 1), 0, SB_DEV - 1).astype(jnp.int32)
    point_coords = jnp.clip(1.0 * jax.random.uniform(part_splits[5], (3, NPTS), jnp.float32) ** steps_of(part_splits[5], (3, NPTS), ((1, 16),), -0.2, 0.2), 0.0, 1.0)
    point_normal = jnp.clip(jax.random.uniform(part_splits[6], (3, NPTS), jnp.float32, -1.0, 1.0) * steps_of(part_splits[6], (3, NPTS), ((1, 16),), -0.4, 0.0), -1.0, 1.0)
    node_coords = jnp.clip(1.0 * jax.random.uniform(part_splits[7], (3, NODES), jnp.float32) ** steps_of(part_splits[7], (3, NODES), ((1, 16),), -0.2, 0.2), 0.0, 1.0)
    struct_prev = bell_draw(part_splits[8], (3, NODES), 1.0, 6.0, ((1, 16),), jnp.float32)
    compliance = jnp.clip(jnp.exp(math.log(2.0) - 1.3862944 * jax.random.uniform(part_splits[9], (NODES,), jnp.float32) ** steps_of(part_splits[9], (NODES,), ((0, 16),), -0.2, 0.2)), 0.5, 2.0)
    elem_nodes = plant(jax.random.randint(part_splits[10], (4, NELEM), 0, NODE_DEV), jax.random.fold_in(part_splits[10], 1), 0, NODE_DEV - 1).astype(jnp.int32)
    elem_stiff = bell_draw(part_splits[11], (12, 12, NELEM), 12 ** -0.5, 1.75, ((2, 16),), jnp.float32)
    iterate = draw_iterate(jax.random.fold_in(jax.random.fold_in(key_of[17], part), 71), part)
    resid_prev = bell_draw(part_splits[13], (3, NPTS), 1.0, 6.0, ((1, 16),), jnp.float32)
    image_prev = bell_draw(part_splits[14], (3, NPTS), 1.0, 6.0, ((1, 16),), jnp.float32)
    resid_history = draw_resid_history(jax.random.fold_in(jax.random.fold_in(key_of[17], part), 71), part)
    image_history = bell_draw(part_splits[16], (HIST, 3, NPTS), 1.0, 6.0, ((2, 16),), jnp.float32)
    return dict(populations=populations, solid_mask=solid_mask, point_cell=point_cell, point_owner=point_owner, point_block=point_block, point_coords=point_coords, point_normal=point_normal, node_coords=node_coords, struct_prev=struct_prev, compliance=compliance, elem_nodes=elem_nodes, elem_stiff=elem_stiff, iterate=iterate, resid_prev=resid_prev, image_prev=image_prev, resid_history=resid_history, image_history=image_history)


velocities = np.array([[0, 0, 0], [1, 0, 0], [-1, 0, 0], [0, 1, 0], [0, -1, 0], [0, 0, 1], [0, 0, -1],
                       [1, 1, 0], [-1, -1, 0], [1, -1, 0], [-1, 1, 0], [1, 0, 1], [-1, 0, -1],
                       [1, 0, -1], [-1, 0, 1], [0, 1, 1], [0, -1, -1], [0, 1, -1], [0, -1, 1]])
lattice_weights = np.array([1.0 / 3.0] + [1.0 / 18.0] * 6 + [1.0 / 36.0] * 12)
opposite = np.array([0, 2, 1, 4, 3, 6, 5, 8, 7, 10, 9, 12, 11, 14, 13, 16, 15, 18, 17])
relax_rate = 1.25
base_density = 19.0
support_scale = 0.1
highest = lax.Precision.HIGHEST


def moments(field):
    table = jnp.asarray(velocities.T, dtype=field.dtype)
    density = jnp.sum(field, axis=0)
    momentum = jnp.tensordot(table, field, axes=1, precision=highest)
    return density, momentum


def collide(populations, solid_mask):
    density, momentum = moments(populations)
    speed = momentum / density
    square = jnp.sum(speed * speed, axis=0)
    relaxed = []
    for direction in range(19):
        step_x = float(velocities[direction, 0])
        step_y = float(velocities[direction, 1])
        step_z = float(velocities[direction, 2])
        project = step_x * speed[0] + step_y * speed[1] + step_z * speed[2]
        weight = float(lattice_weights[direction])
        balance = weight * density * (1.0 + 3.0 * project + 4.5 * project * project - 1.5 * square)
        moved = populations[direction] - relax_rate * (populations[direction] - balance)
        relaxed.append(jnp.where(solid_mask == 1, populations[int(opposite[direction])], moved))
    return relaxed


def rbf_weights(coords, support):
    offset = support - coords[:, :, None]
    distance = jnp.sum(offset * offset, axis=0)
    kernel = 1.0 / (1.0 + distance / support_scale)
    return kernel / jnp.sum(kernel, axis=-1, keepdims=True)


def element_force(field, nodes, stiff):
    gathered = field[:, nodes]
    local_dofs = gathered.transpose(1, 0, 2).reshape(12, -1)
    force = jnp.einsum('ije,je->ie', stiff, local_dofs, precision=highest).reshape(4, 3, -1)
    total = jnp.zeros_like(field)
    for corner in range(4):
        total = total.at[:, nodes[corner]].add(force[corner])
    return total


def solve_small(matrix, rhs):
    size = matrix.shape[0]
    for pivot in range(size):
        scale = matrix[pivot, pivot]
        row_vals = matrix[pivot] / scale
        value = rhs[pivot] / scale
        column = matrix[:, pivot].at[pivot].set(0.0)
        matrix = matrix - column[:, None] * row_vals[None, :]
        matrix = matrix.at[pivot].set(row_vals)
        rhs = rhs - column * value
        rhs = rhs.at[pivot].set(value)
    return rhs


def reference(populations, solid_mask, point_cell, point_owner, point_block, point_coords, point_normal,
              node_coords, struct_prev, compliance, elem_nodes, elem_stiff, iterate, resid_prev, image_prev,
              resid_history, image_history):
    relaxed = collide(populations, solid_mask)
    moved = []
    for direction in range(19):
        step_x = int(velocities[direction, 0])
        step_y = int(velocities[direction, 1])
        step_z = int(velocities[direction, 2])
        moved.append(jnp.roll(relaxed[direction], (step_z, step_x, step_y), axis=(0, 1, 2)))
    populations_next = jnp.stack(moved)

    devices = N_SLAB * N_SIDE
    blocked = populations_next.reshape(19, N_SLAB, LZ_DEV, N_SIDE, LX_DEV, NY)
    blocked = blocked.transpose(0, 1, 3, 2, 4, 5).reshape(19, devices, LZ_DEV * LX_DEV * NY)
    point_device = (jnp.arange(NPTS) // IP_DEV).astype(jnp.int32)
    sampled = blocked[:, point_device, point_cell]
    density, momentum = moments(sampled)
    traction = (density - base_density) / 3.0 * point_normal + momentum

    target = (point_owner[:, 0] * SB_DEV + point_block).astype(jnp.int32)
    node_blocks = node_coords.reshape(3, -1, RBF_BLOCK)

    def split(array):
        return array.reshape(array.shape[0], devices, IP_DEV).transpose(1, 0, 2)

    def accumulate(load, inputs):
        coords, force, block = inputs
        weights = rbf_weights(coords, node_blocks[:, block, :])
        return load.at[:, block, :].add(force[:, :, None] * weights[None]), 0.0

    start = jnp.zeros((3, node_blocks.shape[1], RBF_BLOCK), jnp.float32)
    load, ignored = lax.scan(accumulate, start, (split(point_coords), split(traction), target.reshape(devices, IP_DEV)))
    load = load.reshape(3, -1)

    owner_base = ((jnp.arange(NELEM) // NODE_DEV) * NODE_DEV).astype(jnp.int32)
    global_nodes = elem_nodes + owner_base[None, :]
    stiff_force = element_force(struct_prev, global_nodes, elem_stiff)
    struct_disp = struct_prev + compliance * (load - stiff_force)

    disp_blocks = struct_disp.reshape(3, -1, RBF_BLOCK)

    def sample(inputs):
        coords, block = inputs
        weights = rbf_weights(coords, node_blocks[:, block, :])
        return jnp.sum(disp_blocks[:, block, :] * weights[None], axis=-1)

    image = lax.map(sample, (split(point_coords), target.reshape(devices, IP_DEV)))
    image = image.transpose(1, 0, 2).reshape(3, NPTS)

    resid = image - iterate
    fresh_resid = resid - resid_prev
    fresh_image = image - image_prev
    columns = jnp.concatenate([fresh_resid[None], resid_history], axis=0)
    columns = columns.reshape(columns.shape[0], -1)
    images = jnp.concatenate([fresh_image[None], image_history], axis=0)
    gram = jnp.dot(columns, columns.T, precision=highest)
    rhs = jnp.dot(columns, resid.reshape(-1), precision=highest)
    coeffs = solve_small(gram, -rhs)
    iterate_next = image + jnp.einsum('m,mki->ki', coeffs, images, precision=highest)
    return populations_next, struct_disp, iterate_next
```

```python
import functools

import jax
import jax.numpy as jnp
import numpy as np
from jax import lax
from jax.experimental import pallas as pl
from jax.experimental.pallas import tpu as pltpu
from jax.sharding import PartitionSpec as P

MESH = pl.DeviceIdType.MESH
BLOCK = 128
SUB = 8
PAD = 8
HALO_SLOTS = 8

velocities = np.array(
    [
        [0, 0, 0],
        [1, 0, 0],
        [-1, 0, 0],
        [0, 1, 0],
        [0, -1, 0],
        [0, 0, 1],
        [0, 0, -1],
        [1, 1, 0],
        [-1, -1, 0],
        [1, -1, 0],
        [-1, 1, 0],
        [1, 0, 1],
        [-1, 0, -1],
        [1, 0, -1],
        [-1, 0, 1],
        [0, 1, 1],
        [0, -1, -1],
        [0, 1, -1],
        [0, -1, 1],
    ]
)
lattice_weights = [1.0 / 3.0] + [1.0 / 18.0] * 6 + [1.0 / 36.0] * 12
relax_rate = 1.25
base_density = 19.0
support_scale = 0.1
f32, bf16 = jnp.float32, jnp.bfloat16

z_dirs = {s: [d for d in range(19) if velocities[d, 2] == s] for s in (1, -1)}
x_dirs = {s: [d for d in range(19) if velocities[d, 0] == s] for s in (1, -1)}
corners = [
    (d, int(velocities[d, 0]), int(velocities[d, 2]))
    for d in range(19)
    if velocities[d, 0] != 0 and velocities[d, 2] != 0
]


def pieces(x, count):
    out = []
    for _ in range(count - 1):
        part = x.astype(bf16)
        out.append(part)
        x = x - part.astype(f32)
    out.append(x.astype(bf16))
    return out


def stacked_pieces(x, count):
    out = []
    for _ in range(count - 1):
        part = x.astype(bf16).astype(f32)
        out.append(part)
        x = x - part
    out.append(x)
    return jnp.concatenate(out, axis=0).astype(bf16)


def mm(a, b):
    return jnp.dot(a, b, preferred_element_type=f32)


def mm_nt(a, b):
    return lax.dot_general(a, b, (((1,), (1,)), ((), ())), preferred_element_type=f32)


def rows_iota(rows, columns):
    return lax.broadcasted_iota(jnp.int32, (rows, columns), 0)


def onehot(index, rows):
    return jnp.where(rows_iota(rows, index.shape[1]) == index, 1.0, 0.0).astype(f32)


def fold_lanes(x):
    total = x[:, 0:128]
    for j in range(1, x.shape[1] // 128):
        total = total + x[:, j * 128 : (j + 1) * 128]
    return jnp.sum(total, axis=0, keepdims=True)


def kernel(
    n_slab,
    n_side,
    pop,
    mask,
    cell,
    owner,
    block,
    coords,
    normal,
    nodes,
    sprev,
    comp,
    enodes,
    stiff,
    iterate,
    rprev,
    iprev,
    rhist,
    ihist,
    out_pop,
    out_disp,
    out_iter,
    padded,
    fields,
    zsend,
    zrecv,
    xsend,
    xrecv,
    csend,
    crecv,
    nbuf,
    lsend,
    lrecv,
    dbuf,
    gbuf,
    wide,
    spb,
    dofs,
    force,
    stiffed,
    whi,
    wlo,
    tract,
    image,
    send_sem,
    recv_sem,
    hsend_sem,
    hrecv_sem,
):
    n = n_slab * n_side
    slab = lax.axis_index("slab")
    side = lax.axis_index("side")
    me = slab * n_side + side
    depth, width, span = pop.shape[1:]
    points = cell.shape[1]
    nblocks = n * SUB
    hist = rhist.shape[0]

    def dev(index):
        return {"slab": index // n_side, "side": index % n_side}

    barrier = pltpu.get_barrier_semaphore()

    def greet(o, carry):
        pl.semaphore_signal(barrier, inc=1, device_id=dev((me + o) % n), device_id_type=MESH)
        return carry

    lax.fori_loop(1, n, greet, 0)

    for hi in range(SUB):
        nbuf[me, :, hi, :] = nodes[:, hi * 128 : (hi + 1) * 128]
        spb[:, hi, :] = sprev[:, hi * 128 : (hi + 1) * 128]
    pl.semaphore_wait(barrier, n - 1)

    def exchange(stage, source, target):
        def one(o, carry):
            peer = (me + o) % n
            pltpu.make_async_remote_copy(
                src_ref=source(peer),
                dst_ref=target.at[me],
                send_sem=send_sem.at[stage, peer],
                recv_sem=recv_sem.at[stage, me],
                device_id=dev(peer),
                device_id_type=MESH,
            ).start()
            return carry

        lax.fori_loop(1, n, one, 0)

    def arrived(stage, target):
        def one(o, carry):
            peer = (me + o) % n
            pltpu.make_async_remote_copy(
                src_ref=target.at[peer],
                dst_ref=target.at[peer],
                send_sem=send_sem.at[stage, peer],
                recv_sem=recv_sem.at[stage, peer],
                device_id=dev(peer),
                device_id_type=MESH,
            ).wait_recv()
            return carry

        lax.fori_loop(1, n, one, 0)

    def departed(stage, source):
        def one(o, carry):
            peer = (me + o) % n
            pltpu.make_async_remote_copy(
                src_ref=source(peer),
                dst_ref=source(peer),
                send_sem=send_sem.at[stage, peer],
                recv_sem=recv_sem.at[stage, peer],
                device_id=dev(peer),
                device_id_type=MESH,
            ).wait_send()
            return carry

        lax.fori_loop(1, n, one, 0)

    exchange(0, lambda peer: nbuf.at[me], nbuf)

    chunks = width // 8

    def collide(i, carry):
        z = i // chunks
        x = pl.multiple_of((i % chunks) * 8, 8)
        xp = pl.multiple_of((i % chunks) * 8 + PAD, 8)
        f = [pop[d, z, pl.ds(x, 8), :] for d in range(19)]
        solid = mask[z, pl.ds(x, 8), :] == 1
        density = f[0]
        mom = [None, None, None]
        for d in range(1, 19, 2):
            density = density + (f[d] + f[d + 1])
            diff = f[d] - f[d + 1]
            for axis in range(3):
                c = int(velocities[d, axis])
                if c:
                    if mom[axis] is None:
                        mom[axis] = diff if c > 0 else -diff
                    else:
                        mom[axis] = mom[axis] + diff if c > 0 else mom[axis] - diff
        inv = 1.0 / density
        u = [m * inv for m in mom]
        base = 1.0 - 1.5 * (u[0] * u[0] + u[1] * u[1] + u[2] * u[2])
        keep = 1.0 - relax_rate
        weighted = density * (relax_rate * lattice_weights[0])
        padded[0, z + 1, pl.ds(xp, 8), :] = jnp.where(solid, f[0], keep * f[0] + weighted * base)
        scaled = {w: density * (relax_rate * w) for w in (1.0 / 18.0, 1.0 / 36.0)}
        for d in range(1, 19, 2):
            project = None
            for axis in range(3):
                c = int(velocities[d, axis])
                if c:
                    if project is None:
                        project = u[axis] if c > 0 else -u[axis]
                    else:
                        project = project + u[axis] if c > 0 else project - u[axis]
            w = scaled[lattice_weights[d]]
            even = w * (base + 4.5 * project * project)
            odd = w * (3.0 * project)
            padded[d, z + 1, pl.ds(xp, 8), :] = jnp.where(
                solid, f[d + 1], keep * f[d] + (even + odd)
            )
            padded[d + 1, z + 1, pl.ds(xp, 8), :] = jnp.where(
                solid, f[d], keep * f[d + 1] + (even - odd)
            )
        return carry

    lax.fori_loop(0, depth * chunks, collide, 0)

    halos = []
    for slot, s in enumerate((1, -1)):
        plane = depth if s > 0 else 1
        for j, d in enumerate(z_dirs[s]):
            zsend[slot, j] = padded[d, plane, PAD : PAD + width, :]
        place = {"slab": (slab + s + n_slab) % n_slab}
        halos.append((zsend.at[slot], zrecv.at[slot], slot, place))
    for slot, s in enumerate((1, -1)):
        row = PAD + width - 1 if s > 0 else PAD
        for j, d in enumerate(x_dirs[s]):
            for z in range(depth):
                xsend[slot, j, z : z + 1, :] = padded[d, 1 + z, row : row + 1, :]
        place = {"side": (side + s + n_side) % n_side}
        halos.append((xsend.at[slot], xrecv.at[slot], 2 + slot, place))
    for slot, (d, sx, sz) in enumerate(corners):
        plane = depth if sz > 0 else 1
        row = PAD + width - 1 if sx > 0 else PAD
        csend[slot] = jnp.broadcast_to(padded[d, plane, row : row + 1, :], (8, span))
        place = {
            "slab": (slab + sz + n_slab) % n_slab,
            "side": (side + sx + n_side) % n_side,
        }
        halos.append((csend.at[slot], crecv.at[slot], 4 + slot, place))
    halo_copies = []
    for source, target, index, place in halos:
        copy = pltpu.make_async_remote_copy(
            src_ref=source,
            dst_ref=target,
            send_sem=hsend_sem.at[index],
            recv_sem=hrecv_sem.at[index],
            device_id=place,
            device_id_type=MESH,
        )
        copy.start()
        halo_copies.append(copy)

    elems = enodes.shape[1]
    prev_pieces = stacked_pieces(spb[...].reshape(3 * SUB, 128), 3)
    rows = 3 * SUB
    for c in range(4):
        ids = enodes[c : c + 1, :]
        low = onehot(ids & 127, 128).astype(bf16)
        high = rows_iota(SUB, elems) == (ids >> 7)
        got = mm(prev_pieces, low)
        got = got[0:rows] + got[rows : 2 * rows] + got[2 * rows : 3 * rows]
        for k in range(3):
            part = jnp.where(high, got[k * SUB : (k + 1) * SUB], 0.0)
            dofs[3 * c + k : 3 * c + k + 1, :] = jnp.sum(part, axis=0, keepdims=True)
    local = dofs[...]
    for i in range(12):
        force[i : i + 1, :] = jnp.sum(stiff[i] * local, axis=0, keepdims=True)
    total = jnp.zeros((3 * rows, 128), f32)
    for c in range(4):
        ids = enodes[c : c + 1, :]
        low = onehot(ids & 127, 128).astype(bf16)
        high = rows_iota(SUB, elems) == (ids >> 7)
        spread = [jnp.where(high, force[3 * c + k : 3 * c + k + 1, :], 0.0) for k in range(3)]
        total = total + mm_nt(stacked_pieces(jnp.concatenate(spread, axis=0), 3), low)
    total = total[0:rows] + total[rows : 2 * rows] + total[2 * rows : 3 * rows]
    stiffed[...] = total.reshape(3, SUB, 128)

    def row_of(i, j):
        return sum(hist + 1 - q for q in range(i)) + (j - i)

    pairs = row_of(hist, hist) + 1
    gbuf[me] = jnp.zeros(gbuf.shape[1:], f32)
    for i in range(hist):
        for j in range(i, hist):
            r = row_of(i + 1, j + 1)
            gbuf[me, r : r + 1, :] = fold_lanes(rhist[i] * rhist[j])

    arrived(0, nbuf)
    step = 512 if nblocks <= 128 else 128
    node_pieces = []
    for k in range(3):
        turned = nbuf[:, k].reshape(nblocks, BLOCK).T
        node_pieces.append(jnp.concatenate(pieces(turned, 3), axis=1))
    wide[...] = jnp.concatenate(node_pieces, axis=0)

    def group_of(at):
        return owner[:, pl.ds(at, step)] * SUB + block[:, pl.ds(at, step)]

    def weigh(i, carry):
        at = pl.multiple_of(i * step, step)
        hot = onehot(group_of(at), nblocks).astype(bf16)
        support = mm(wide[...], jnp.concatenate([hot, hot, hot], axis=0))
        distance = None
        for k in range(3):
            offset = support[k * BLOCK : (k + 1) * BLOCK] - coords[k : k + 1, pl.ds(at, step)]
            square = offset * offset
            distance = square if distance is None else distance + square
        phi = 1.0 / (1.0 + distance * (1.0 / support_scale))
        weight = phi * (1.0 / jnp.sum(phi, axis=0, keepdims=True))
        upper, lower = pieces(weight, 2)
        whi[:, pl.ds(at, step)] = upper
        wlo[:, pl.ds(at, step)] = lower
        return carry

    lax.fori_loop(0, points // step, weigh, 0)

    for copy in halo_copies:
        copy.wait_recv()
    for slot, s in enumerate((1, -1)):
        plane = 0 if s > 0 else depth + 1
        for j, d in enumerate(z_dirs[s]):
            padded[d, plane, PAD : PAD + width, :] = zrecv[slot, j]
    for slot, s in enumerate((1, -1)):
        row = PAD - 1 if s > 0 else PAD + width
        for j, d in enumerate(x_dirs[s]):
            for z in range(depth):
                padded[d, 1 + z, row : row + 1, :] = xrecv[slot, j, z : z + 1, :]
    for slot, (d, sx, sz) in enumerate(corners):
        plane = 0 if sz > 0 else depth + 1
        row = PAD - 1 if sx > 0 else PAD + width
        padded[d, plane, row : row + 1, :] = crecv[slot, 0:1, :]

    def stream(z, carry):
        for x in range(0, width, 16):
            density = None
            mom = [None, None, None]
            for d in range(19):
                cx, cy, cz = (int(v) for v in velocities[d])
                piece = padded[d, z + 1 - cz, PAD + x - cx : PAD + x - cx + 16, :]
                if cy:
                    piece = pltpu.roll(piece, cy % span, 1)
                out_pop[d, z, x : x + 16, :] = piece
                density = piece if density is None else density + piece
                for axis, c in enumerate((cx, cy, cz)):
                    if c:
                        if mom[axis] is None:
                            mom[axis] = piece if c > 0 else -piece
                        else:
                            mom[axis] = mom[axis] + piece if c > 0 else mom[axis] - piece
            where = pl.ds(pl.multiple_of(z * width + x, 16), 16)
            fields[0, where, :] = (density - base_density) * (1.0 / 3.0)
            for axis in range(3):
                fields[1 + axis, where, :] = mom[axis]
        return carry

    lax.fori_loop(0, depth, stream, 0)

    cells = depth * width
    turned = jnp.concatenate([fields[k].T for k in range(4)], axis=0)
    turned_hi, turned_lo = pieces(turned, 2)
    tstep = 512

    def sample(i, carry):
        at = pl.multiple_of(i * tstep, tstep)
        ids = cell[:, pl.ds(at, tstep)]
        hot = onehot(ids // span, cells).astype(bf16)
        picked = mm(turned_hi, hot) + mm(turned_lo, hot)
        chosen = rows_iota(span, tstep) == (ids % span)
        got = []
        for k in range(4):
            part = jnp.where(chosen, picked[k * span : (k + 1) * span], 0.0)
            got.append(jnp.sum(part, axis=0, keepdims=True))
        for k in range(3):
            tract[k : k + 1, pl.ds(at, tstep)] = (
                got[0] * normal[k : k + 1, pl.ds(at, tstep)] + got[1 + k]
            )
        return carry

    lax.fori_loop(0, points // tstep, sample, 0)

    def gather_load(i, total):
        at = pl.multiple_of(i * step, step)
        chosen = rows_iota(nblocks, step) == group_of(at)
        spread = [jnp.where(chosen, tract[k : k + 1, pl.ds(at, step)], 0.0) for k in range(3)]
        upper, lower = pieces(jnp.concatenate(spread, axis=0), 2)
        first, second = whi[:, pl.ds(at, step)], wlo[:, pl.ds(at, step)]
        return total + (mm_nt(upper, first) + (mm_nt(lower, first) + mm_nt(upper, second)))

    load = lax.fori_loop(
        0, points // step, gather_load, jnp.zeros((3 * nblocks, BLOCK), f32)
    )
    for k in range(3):
        lsend[:, k] = load[k * nblocks : (k + 1) * nblocks].reshape(n, SUB, BLOCK)
    exchange(1, lambda peer: lsend.at[peer], lrecv)
    lrecv[me] = lsend[me]
    arrived(1, lrecv)
    load = jnp.sum(lrecv[...], axis=0)

    disp = spb[...] + comp[...][None] * (load - stiffed[...])
    dbuf[me] = disp
    exchange(2, lambda peer: dbuf.at[me], dbuf)
    for hi in range(SUB):
        out_disp[:, hi * 128 : (hi + 1) * 128] = dbuf[me, :, hi, :]
    arrived(2, dbuf)

    field = jnp.concatenate([dbuf[:, k].reshape(nblocks, BLOCK) for k in range(3)], axis=0)
    field_hi, field_lo = pieces(field, 2)

    def map_back(i, carry):
        at = pl.multiple_of(i * step, step)
        first, second = whi[:, pl.ds(at, step)], wlo[:, pl.ds(at, step)]
        mapped = mm(field_hi, first) + (mm(field_lo, first) + mm(field_hi, second))
        chosen = rows_iota(nblocks, step) == group_of(at)
        for k in range(3):
            part = jnp.where(chosen, mapped[k * nblocks : (k + 1) * nblocks], 0.0)
            image[k : k + 1, pl.ds(at, step)] = jnp.sum(part, axis=0, keepdims=True)
        return carry

    lax.fori_loop(0, points // step, map_back, 0)

    resid = image[...] - iterate[...]
    fresh = resid - rprev[...]
    gbuf[me, 0:1, :] = fold_lanes(fresh * fresh)
    gbuf[me, pairs : pairs + 1, :] = fold_lanes(fresh * resid)
    for i in range(hist):
        r = row_of(0, i + 1)
        gbuf[me, r : r + 1, :] = fold_lanes(fresh * rhist[i])
        gbuf[me, pairs + 1 + i : pairs + 2 + i, :] = fold_lanes(resid * rhist[i])
    exchange(3, lambda peer: gbuf.at[me], gbuf)
    arrived(3, gbuf)
    sums = jnp.sum(jnp.sum(gbuf[...], axis=0), axis=1, keepdims=True)
    size = hist + 1

    def entry(r):
        return sums[r : r + 1, 0:1]

    matrix = [[entry(row_of(min(i, j), max(i, j))) for j in range(size)] for i in range(size)]
    rhs = [-entry(pairs + i) for i in range(size)]
    for pivot in range(size):
        scale = 1.0 / matrix[pivot][pivot]
        row_vals = [v * scale for v in matrix[pivot]]
        value = rhs[pivot] * scale
        for i in range(size):
            if i != pivot:
                factor = matrix[i][pivot]
                matrix[i] = [matrix[i][j] - factor * row_vals[j] for j in range(size)]
                rhs[i] = rhs[i] - factor * value
        matrix[pivot], rhs[pivot] = row_vals, value
    result = image[...] + rhs[0] * (image[...] - iprev[...])
    for i in range(hist):
        result = result + rhs[1 + i] * ihist[i]
    out_iter[...] = result

    for copy in halo_copies:
        copy.wait_send()
    departed(0, lambda peer: nbuf.at[me])
    departed(1, lambda peer: lsend.at[peer])
    departed(2, lambda peer: dbuf.at[me])
    departed(3, lambda peer: gbuf.at[me])


def body(n_slab, n_side, *args):
    (
        populations,
        solid_mask,
        point_cell,
        point_owner,
        point_block,
        point_coords,
        point_normal,
        node_coords,
        struct_prev,
        compliance,
        elem_nodes,
        elem_stiff,
        iterate,
        resid_prev,
        image_prev,
        resid_history,
        image_history,
    ) = args
    n = n_slab * n_side
    directions, depth, width, span = populations.shape
    points = point_cell.shape[0]
    elems = elem_nodes.shape[1]
    nblocks = n * SUB
    vmem = pl.BlockSpec(memory_space=pltpu.VMEM)
    DMA = pltpu.SemaphoreType.DMA
    return pl.pallas_call(
        functools.partial(kernel, n_slab, n_side),
        out_shape=(
            jax.ShapeDtypeStruct(populations.shape, f32),
            jax.ShapeDtypeStruct(struct_prev.shape, f32),
            jax.ShapeDtypeStruct(iterate.shape, f32),
        ),
        in_specs=[vmem] * 17,
        out_specs=(vmem, vmem, vmem),
        scratch_shapes=[
            pltpu.VMEM((directions, depth + 2, width + 2 * PAD, span), f32),
            pltpu.VMEM((4, depth * width, span), f32),
            pltpu.VMEM((2, 5, width, span), f32),
            pltpu.VMEM((2, 5, width, span), f32),
            pltpu.VMEM((2, 5, depth, span), f32),
            pltpu.VMEM((2, 5, depth, span), f32),
            pltpu.VMEM((4, 8, span), f32),
            pltpu.VMEM((4, 8, span), f32),
            pltpu.VMEM((n, 3, SUB, BLOCK), f32),
            pltpu.VMEM((n, 3, SUB, BLOCK), f32),
            pltpu.VMEM((n, 3, SUB, BLOCK), f32),
            pltpu.VMEM((n, 3, SUB, BLOCK), f32),
            pltpu.VMEM((n, 24, BLOCK), f32),
            pltpu.VMEM((3 * BLOCK, 3 * nblocks), bf16),
            pltpu.VMEM((3, SUB, BLOCK), f32),
            pltpu.VMEM((12, elems), f32),
            pltpu.VMEM((12, elems), f32),
            pltpu.VMEM((3, SUB, BLOCK), f32),
            pltpu.VMEM((BLOCK, points), bf16),
            pltpu.VMEM((BLOCK, points), bf16),
            pltpu.VMEM((3, points), f32),
            pltpu.VMEM((3, points), f32),
            DMA((4, n)),
            DMA((4, n)),
            DMA((HALO_SLOTS,)),
            DMA((HALO_SLOTS,)),
        ],
        compiler_params=pltpu.CompilerParams(
            collective_id=0, has_side_effects=True, vmem_limit_bytes=52 * 2**20
        ),
    )(
        populations,
        solid_mask,
        point_cell.reshape(1, points),
        point_owner.reshape(1, points),
        point_block.reshape(1, points),
        point_coords,
        point_normal,
        node_coords,
        struct_prev,
        compliance.reshape(SUB, BLOCK),
        elem_nodes,
        elem_stiff,
        iterate,
        resid_prev,
        image_prev,
        resid_history,
        image_history,
    )


def solution(mesh):
    lattice = P(None, ("groups", "slab"), "side", None)
    last = P(None, ("groups", "slab", "side"))
    one = P(("groups", "slab", "side"))
    deep = P(None, None, ("groups", "slab", "side"))
    return jax.shard_map(
        functools.partial(body, mesh.shape["slab"], mesh.shape["side"]),
        mesh=mesh,
        in_specs=(
            P(None, ("groups", "slab"), "side", None),
            P(("groups", "slab"), "side", None),
            one,
            P(("groups", "slab", "side"), None),
            one,
            last,
            last,
            last,
            last,
            one,
            last,
            deep,
            last,
            last,
            last,
            deep,
            deep,
        ),
        out_specs=(lattice, last, last),
        check_vma=False,
    )
```

```python
import functools

import jax
import jax.numpy as jnp
import numpy as np
from jax import lax
from jax.experimental import pallas as pl
from jax.experimental.pallas import tpu as pltpu
from jax.sharding import PartitionSpec as P

MESH = pl.DeviceIdType.MESH
BLOCK = 128
SUB = 8
PAD = 8
HALO_SLOTS = 8

velocities = np.array(
    [
        [0, 0, 0],
        [1, 0, 0],
        [-1, 0, 0],
        [0, 1, 0],
        [0, -1, 0],
        [0, 0, 1],
        [0, 0, -1],
        [1, 1, 0],
        [-1, -1, 0],
        [1, -1, 0],
        [-1, 1, 0],
        [1, 0, 1],
        [-1, 0, -1],
        [1, 0, -1],
        [-1, 0, 1],
        [0, 1, 1],
        [0, -1, -1],
        [0, 1, -1],
        [0, -1, 1],
    ]
)
lattice_weights = [1.0 / 3.0] + [1.0 / 18.0] * 6 + [1.0 / 36.0] * 12
relax_rate = 1.25
base_density = 19.0
support_scale = 0.1
f32, bf16 = jnp.float32, jnp.bfloat16

z_dirs = {s: [d for d in range(19) if velocities[d, 2] == s] for s in (1, -1)}
x_dirs = {s: [d for d in range(19) if velocities[d, 0] == s] for s in (1, -1)}
corners = [
    (d, int(velocities[d, 0]), int(velocities[d, 2]))
    for d in range(19)
    if velocities[d, 0] != 0 and velocities[d, 2] != 0
]


def pieces(x, count):
    out = []
    for _ in range(count - 1):
        part = x.astype(bf16)
        out.append(part)
        x = x - part.astype(f32)
    out.append(x.astype(bf16))
    return out


def stacked_pieces(x, count):
    out = []
    for _ in range(count - 1):
        part = x.astype(bf16).astype(f32)
        out.append(part)
        x = x - part
    out.append(x)
    return jnp.concatenate(out, axis=0).astype(bf16)


def mm(a, b):
    return jnp.dot(a, b, preferred_element_type=f32)


def mm_nt(a, b):
    return lax.dot_general(a, b, (((1,), (1,)), ((), ())), preferred_element_type=f32)


def rows_iota(rows, columns):
    return lax.broadcasted_iota(jnp.int32, (rows, columns), 0)


def onehot(index, rows):
    return jnp.where(rows_iota(rows, index.shape[1]) == index, 1.0, 0.0).astype(f32)


def fold_lanes(x):
    total = x[:, 0:128]
    for j in range(1, x.shape[1] // 128):
        total = total + x[:, j * 128 : (j + 1) * 128]
    return jnp.sum(total, axis=0, keepdims=True)


def kernel(
    n_slab,
    n_side,
    pop_in,
    mask_in,
    cell_in,
    owner_in,
    block_in,
    coords_in,
    normal_in,
    nodes_in,
    sprev_in,
    comp_in,
    enodes_in,
    stiff_in,
    iterate_in,
    rprev_in,
    iprev_in,
    rhist_in,
    ihist_in,
    out_pop,
    out_disp,
    out_iter,
    padded,
    fields,
    zsend,
    zrecv,
    xsend,
    xrecv,
    csend,
    crecv,
    nbuf,
    lsend,
    lrecv,
    dbuf,
    gbuf,
    wide,
    spb,
    dofs,
    force,
    stiffed,
    whi,
    wlo,
    tract,
    image,
    send_sem,
    recv_sem,
    hsend_sem,
    hrecv_sem,
    vcols,
    wcols,
    load_sem,
    pop,
    mask,
    cell,
    owner,
    block,
    coords,
    normal,
    nodes,
    sprev,
    comp,
    enodes,
    stiff,
    iterate,
    rprev,
    iprev,
    rhist,
    ihist,
):
    n = n_slab * n_side
    slab = lax.axis_index("slab")
    side = lax.axis_index("side")
    me = slab * n_side + side
    depth, width, span = pop.shape[1:]
    points = cell.shape[1]
    nblocks = n * SUB
    hist = rhist.shape[1]

    order = ("nodes", "sprev", "pop", "mask", "enodes", "stiff", "owner", "block", "coords")
    order += ("rhist", "ihist", "comp", "cell", "normal", "iterate", "rprev", "iprev")
    held = dict(
        pop=(pop_in, pop),
        mask=(mask_in, mask),
        cell=(cell_in, cell),
        owner=(owner_in, owner),
        block=(block_in, block),
        coords=(coords_in, coords),
        normal=(normal_in, normal),
        nodes=(nodes_in, nodes),
        sprev=(sprev_in, sprev),
        comp=(comp_in, comp),
        enodes=(enodes_in, enodes),
        stiff=(stiff_in, stiff),
        iterate=(iterate_in, iterate),
        rprev=(rprev_in, rprev),
        iprev=(iprev_in, iprev),
        rhist=(rhist_in, rhist),
        ihist=(ihist_in, ihist),
    )
    loads = {}
    for place, name in enumerate(order):
        loads[name] = pltpu.make_async_copy(*held[name], load_sem.at[place])
        loads[name].start()

    def ready(*names):
        for name in names:
            loads[name].wait()

    def dev(index):
        return {"slab": index // n_side, "side": index % n_side}

    barrier = pltpu.get_barrier_semaphore()

    def greet(o, carry):
        pl.semaphore_signal(barrier, inc=1, device_id=dev((me + o) % n), device_id_type=MESH)
        return carry

    lax.fori_loop(1, n, greet, 0)

    ready("nodes", "sprev")
    for hi in range(SUB):
        nbuf[me, :, hi, :] = nodes[:, hi * 128 : (hi + 1) * 128]
        spb[:, hi, :] = sprev[:, hi * 128 : (hi + 1) * 128]
    pl.semaphore_wait(barrier, n - 1)

    def exchange(stage, source, target):
        def one(o, carry):
            peer = (me + o) % n
            pltpu.make_async_remote_copy(
                src_ref=source(peer),
                dst_ref=target.at[me],
                send_sem=send_sem.at[stage, peer],
                recv_sem=recv_sem.at[stage, me],
                device_id=dev(peer),
                device_id_type=MESH,
            ).start()
            return carry

        lax.fori_loop(1, n, one, 0)

    def arrived(stage, target):
        def one(o, carry):
            peer = (me + o) % n
            pltpu.make_async_remote_copy(
                src_ref=target.at[peer],
                dst_ref=target.at[peer],
                send_sem=send_sem.at[stage, peer],
                recv_sem=recv_sem.at[stage, peer],
                device_id=dev(peer),
                device_id_type=MESH,
            ).wait_recv()
            return carry

        lax.fori_loop(1, n, one, 0)

    def departed(stage, source):
        def one(o, carry):
            peer = (me + o) % n
            pltpu.make_async_remote_copy(
                src_ref=source(peer),
                dst_ref=source(peer),
                send_sem=send_sem.at[stage, peer],
                recv_sem=recv_sem.at[stage, peer],
                device_id=dev(peer),
                device_id_type=MESH,
            ).wait_send()
            return carry

        lax.fori_loop(1, n, one, 0)

    exchange(0, lambda peer: nbuf.at[me], nbuf)

    ready("pop", "mask")
    chunks = width // 8

    def collide(i, carry):
        z = i // chunks
        x = pl.multiple_of((i % chunks) * 8, 8)
        xp = pl.multiple_of((i % chunks) * 8 + PAD, 8)
        f = [pop[d, z, pl.ds(x, 8), :] for d in range(19)]
        solid = mask[z, pl.ds(x, 8), :] == 1
        density = f[0]
        mom = [None, None, None]
        for d in range(1, 19, 2):
            density = density + (f[d] + f[d + 1])
            diff = f[d] - f[d + 1]
            for axis in range(3):
                c = int(velocities[d, axis])
                if c:
                    if mom[axis] is None:
                        mom[axis] = diff if c > 0 else -diff
                    else:
                        mom[axis] = mom[axis] + diff if c > 0 else mom[axis] - diff
        inv = 1.0 / density
        u = [m * inv for m in mom]
        base = 1.0 - 1.5 * (u[0] * u[0] + u[1] * u[1] + u[2] * u[2])
        keep = 1.0 - relax_rate
        weighted = density * (relax_rate * lattice_weights[0])
        padded[0, z + 1, pl.ds(xp, 8), :] = jnp.where(solid, f[0], keep * f[0] + weighted * base)
        scaled = {w: density * (relax_rate * w) for w in (1.0 / 18.0, 1.0 / 36.0)}
        for d in range(1, 19, 2):
            project = None
            for axis in range(3):
                c = int(velocities[d, axis])
                if c:
                    if project is None:
                        project = u[axis] if c > 0 else -u[axis]
                    else:
                        project = project + u[axis] if c > 0 else project - u[axis]
            w = scaled[lattice_weights[d]]
            even = w * (base + 4.5 * project * project)
            odd = w * (3.0 * project)
            padded[d, z + 1, pl.ds(xp, 8), :] = jnp.where(
                solid, f[d + 1], keep * f[d] + (even + odd)
            )
            padded[d + 1, z + 1, pl.ds(xp, 8), :] = jnp.where(
                solid, f[d], keep * f[d + 1] + (even - odd)
            )
        return carry

    lax.fori_loop(0, depth * chunks, collide, 0)

    halos = []
    for slot, s in enumerate((1, -1)):
        plane = depth if s > 0 else 1
        for j, d in enumerate(z_dirs[s]):
            zsend[slot, j] = padded[d, plane, PAD : PAD + width, :]
        place = {"slab": (slab + s + n_slab) % n_slab}
        halos.append((zsend.at[slot], zrecv.at[slot], slot, place))
    for slot, s in enumerate((1, -1)):
        row = PAD + width - 1 if s > 0 else PAD
        for j, d in enumerate(x_dirs[s]):
            for z in range(depth):
                xsend[slot, j, z : z + 1, :] = padded[d, 1 + z, row : row + 1, :]
        place = {"side": (side + s + n_side) % n_side}
        halos.append((xsend.at[slot], xrecv.at[slot], 2 + slot, place))
    for slot, (d, sx, sz) in enumerate(corners):
        plane = depth if sz > 0 else 1
        row = PAD + width - 1 if sx > 0 else PAD
        csend[slot] = jnp.broadcast_to(padded[d, plane, row : row + 1, :], (8, span))
        place = {
            "slab": (slab + sz + n_slab) % n_slab,
            "side": (side + sx + n_side) % n_side,
        }
        halos.append((csend.at[slot], crecv.at[slot], 4 + slot, place))
    halo_copies = []
    for source, target, index, place in halos:
        copy = pltpu.make_async_remote_copy(
            src_ref=source,
            dst_ref=target,
            send_sem=hsend_sem.at[index],
            recv_sem=hrecv_sem.at[index],
            device_id=place,
            device_id_type=MESH,
        )
        copy.start()
        halo_copies.append(copy)

    ready("enodes", "stiff")
    elems = enodes.shape[1]
    prev_pieces = stacked_pieces(spb[...].reshape(3 * SUB, 128), 3)
    rows = 3 * SUB
    for c in range(4):
        ids = enodes[c : c + 1, :]
        low = onehot(ids & 127, 128).astype(bf16)
        high = rows_iota(SUB, elems) == (ids >> 7)
        got = mm(prev_pieces, low)
        got = got[0:rows] + got[rows : 2 * rows] + got[2 * rows : 3 * rows]
        for k in range(3):
            part = jnp.where(high, got[k * SUB : (k + 1) * SUB], 0.0)
            dofs[3 * c + k : 3 * c + k + 1, :] = jnp.sum(part, axis=0, keepdims=True)
    local = dofs[...]
    for i in range(12):
        force[i : i + 1, :] = jnp.sum(stiff[i] * local, axis=0, keepdims=True)
    total = jnp.zeros((3 * rows, 128), f32)
    for c in range(4):
        ids = enodes[c : c + 1, :]
        low = onehot(ids & 127, 128).astype(bf16)
        high = rows_iota(SUB, elems) == (ids >> 7)
        spread = [jnp.where(high, force[3 * c + k : 3 * c + k + 1, :], 0.0) for k in range(3)]
        total = total + mm_nt(stacked_pieces(jnp.concatenate(spread, axis=0), 3), low)
    total = total[0:rows] + total[rows : 2 * rows] + total[2 * rows : 3 * rows]
    stiffed[...] = total.reshape(3, SUB, 128)

    ready("rhist", "ihist")
    for k in range(3):
        vcols[k] = jnp.zeros(vcols.shape[1:], f32)
        wcols[k] = jnp.zeros(wcols.shape[1:], f32)
        vcols[k, 1 : 1 + hist, :] = rhist[k]
        wcols[k, 1 : 1 + hist, :] = ihist[k]

    ready("owner", "block", "coords")
    arrived(0, nbuf)
    step = 512 if nblocks <= 128 else 128
    node_pieces = []
    for k in range(3):
        turned = nbuf[:, k].reshape(nblocks, BLOCK).T
        node_pieces.append(jnp.concatenate(pieces(turned, 3), axis=1))
    wide[...] = jnp.concatenate(node_pieces, axis=0)

    def group_of(at):
        return owner[:, pl.ds(at, step)] * SUB + block[:, pl.ds(at, step)]

    def weigh(i, carry):
        at = pl.multiple_of(i * step, step)
        hot = onehot(group_of(at), nblocks).astype(bf16)
        support = mm(wide[...], jnp.concatenate([hot, hot, hot], axis=0))
        distance = None
        for k in range(3):
            offset = support[k * BLOCK : (k + 1) * BLOCK] - coords[k : k + 1, pl.ds(at, step)]
            square = offset * offset
            distance = square if distance is None else distance + square
        phi = 1.0 / (1.0 + distance * (1.0 / support_scale))
        weight = phi * (1.0 / jnp.sum(phi, axis=0, keepdims=True))
        upper, lower = pieces(weight, 2)
        whi[:, pl.ds(at, step)] = upper
        wlo[:, pl.ds(at, step)] = lower
        return carry

    lax.fori_loop(0, points // step, weigh, 0)

    for copy in halo_copies:
        copy.wait_recv()
    for slot, s in enumerate((1, -1)):
        plane = 0 if s > 0 else depth + 1
        for j, d in enumerate(z_dirs[s]):
            padded[d, plane, PAD : PAD + width, :] = zrecv[slot, j]
    for slot, s in enumerate((1, -1)):
        row = PAD - 1 if s > 0 else PAD + width
        for j, d in enumerate(x_dirs[s]):
            for z in range(depth):
                padded[d, 1 + z, row : row + 1, :] = xrecv[slot, j, z : z + 1, :]
    for slot, (d, sx, sz) in enumerate(corners):
        plane = 0 if sz > 0 else depth + 1
        row = PAD - 1 if sx > 0 else PAD + width
        padded[d, plane, row : row + 1, :] = crecv[slot, 0:1, :]

    def stream(z, carry):
        for x in range(0, width, 16):
            density = None
            mom = [None, None, None]
            for d in range(19):
                cx, cy, cz = (int(v) for v in velocities[d])
                piece = padded[d, z + 1 - cz, PAD + x - cx : PAD + x - cx + 16, :]
                if cy:
                    piece = pltpu.roll(piece, cy % span, 1)
                out_pop[d, z, x : x + 16, :] = piece
                density = piece if density is None else density + piece
                for axis, c in enumerate((cx, cy, cz)):
                    if c:
                        if mom[axis] is None:
                            mom[axis] = piece if c > 0 else -piece
                        else:
                            mom[axis] = mom[axis] + piece if c > 0 else mom[axis] - piece
            where = pl.ds(pl.multiple_of(z * width + x, 16), 16)
            fields[0, where, :] = (density - base_density) * (1.0 / 3.0)
            for axis in range(3):
                fields[1 + axis, where, :] = mom[axis]
        return carry

    lax.fori_loop(0, depth, stream, 0)

    ready("cell", "normal")
    cells = depth * width
    turned = jnp.concatenate([fields[k].T for k in range(4)], axis=0)
    turned_hi, turned_lo = pieces(turned, 2)
    tstep = 512

    def sample(i, carry):
        at = pl.multiple_of(i * tstep, tstep)
        ids = cell[:, pl.ds(at, tstep)]
        hot = onehot(ids // span, cells).astype(bf16)
        picked = mm(turned_hi, hot) + mm(turned_lo, hot)
        chosen = rows_iota(span, tstep) == (ids % span)
        got = []
        for k in range(4):
            part = jnp.where(chosen, picked[k * span : (k + 1) * span], 0.0)
            got.append(jnp.sum(part, axis=0, keepdims=True))
        for k in range(3):
            tract[k : k + 1, pl.ds(at, tstep)] = (
                got[0] * normal[k : k + 1, pl.ds(at, tstep)] + got[1 + k]
            )
        return carry

    lax.fori_loop(0, points // tstep, sample, 0)

    def gather_load(i, total):
        at = pl.multiple_of(i * step, step)
        chosen = rows_iota(nblocks, step) == group_of(at)
        spread = [jnp.where(chosen, tract[k : k + 1, pl.ds(at, step)], 0.0) for k in range(3)]
        upper, lower = pieces(jnp.concatenate(spread, axis=0), 2)
        first, second = whi[:, pl.ds(at, step)], wlo[:, pl.ds(at, step)]
        return total + (mm_nt(upper, first) + (mm_nt(lower, first) + mm_nt(upper, second)))

    load = lax.fori_loop(
        0, points // step, gather_load, jnp.zeros((3 * nblocks, BLOCK), f32)
    )
    for k in range(3):
        lsend[:, k] = load[k * nblocks : (k + 1) * nblocks].reshape(n, SUB, BLOCK)
    exchange(1, lambda peer: lsend.at[peer], lrecv)
    lrecv[me] = lsend[me]
    arrived(1, lrecv)
    load = jnp.sum(lrecv[...], axis=0)

    ready("comp")
    disp = spb[...] + comp[...][None] * (load - stiffed[...])
    dbuf[me] = disp
    exchange(2, lambda peer: dbuf.at[me], dbuf)
    for hi in range(SUB):
        out_disp[:, hi * 128 : (hi + 1) * 128] = dbuf[me, :, hi, :]
    arrived(2, dbuf)

    field = jnp.concatenate([dbuf[:, k].reshape(nblocks, BLOCK) for k in range(3)], axis=0)
    field_hi, field_lo = pieces(field, 2)

    def map_back(i, carry):
        at = pl.multiple_of(i * step, step)
        first, second = whi[:, pl.ds(at, step)], wlo[:, pl.ds(at, step)]
        mapped = mm(field_hi, first) + (mm(field_lo, first) + mm(field_hi, second))
        chosen = rows_iota(nblocks, step) == group_of(at)
        for k in range(3):
            part = jnp.where(chosen, mapped[k * nblocks : (k + 1) * nblocks], 0.0)
            image[k : k + 1, pl.ds(at, step)] = jnp.sum(part, axis=0, keepdims=True)
        return carry

    lax.fori_loop(0, points // step, map_back, 0)

    ready("iterate", "rprev", "iprev")
    gram = None
    for k in range(3):
        now = image[k : k + 1, :]
        resid = now - iterate[k : k + 1, :]
        vcols[k, 0:1, :] = resid - rprev[k : k + 1, :]
        vcols[k, 1 + hist : 2 + hist, :] = resid
        wcols[k, 0:1, :] = now - iprev[k : k + 1, :]
        parts = stacked_pieces(vcols[k], 3)
        term = mm_nt(parts, parts)
        gram = term if gram is None else gram + term
    gram = gram[0:8] + gram[8:16] + gram[16:24]
    gram = gram[:, 0:8] + gram[:, 8:16] + gram[:, 16:24]
    gbuf[me] = jnp.concatenate([gram, jnp.zeros((8, BLOCK - 8), f32)], axis=1)
    exchange(3, lambda peer: gbuf.at[me], gbuf)
    arrived(3, gbuf)
    sums = jnp.sum(gbuf[...], axis=0)
    size = hist + 1

    matrix = [[sums[i : i + 1, j : j + 1] for j in range(size)] for i in range(size)]
    rhs = [-sums[i : i + 1, size : size + 1] for i in range(size)]
    for pivot in range(size):
        scale = 1.0 / matrix[pivot][pivot]
        row_vals = [v * scale for v in matrix[pivot]]
        value = rhs[pivot] * scale
        for i in range(size):
            if i != pivot:
                factor = matrix[i][pivot]
                matrix[i] = [matrix[i][j] - factor * row_vals[j] for j in range(size)]
                rhs[i] = rhs[i] - factor * value
        matrix[pivot], rhs[pivot] = row_vals, value
    coeffs = jnp.concatenate(rhs + [jnp.zeros((8 - size, 1), f32)], axis=0)
    for k in range(3):
        change = jnp.sum(wcols[k] * coeffs, axis=0, keepdims=True)
        out_iter[k : k + 1, :] = image[k : k + 1, :] + change

    for copy in halo_copies:
        copy.wait_send()
    departed(0, lambda peer: nbuf.at[me])
    departed(1, lambda peer: lsend.at[peer])
    departed(2, lambda peer: dbuf.at[me])
    departed(3, lambda peer: gbuf.at[me])


def body(n_slab, n_side, *args):
    (
        populations,
        solid_mask,
        point_cell,
        point_owner,
        point_block,
        point_coords,
        point_normal,
        node_coords,
        struct_prev,
        compliance,
        elem_nodes,
        elem_stiff,
        iterate,
        resid_prev,
        image_prev,
        resid_history,
        image_history,
    ) = args
    n = n_slab * n_side
    directions, depth, width, span = populations.shape
    points = point_cell.shape[0]
    elems = elem_nodes.shape[1]
    nblocks = n * SUB
    vmem = pl.BlockSpec(memory_space=pltpu.VMEM)
    DMA = pltpu.SemaphoreType.DMA
    operands = (
        populations,
        solid_mask,
        point_cell.reshape(1, points),
        point_owner.reshape(1, points),
        point_block.reshape(1, points),
        point_coords,
        point_normal,
        node_coords,
        struct_prev,
        compliance.reshape(SUB, BLOCK),
        elem_nodes,
        elem_stiff,
        iterate,
        resid_prev,
        image_prev,
        resid_history.transpose(1, 0, 2),
        image_history.transpose(1, 0, 2),
    )
    return pl.pallas_call(
        functools.partial(kernel, n_slab, n_side),
        out_shape=(
            jax.ShapeDtypeStruct(populations.shape, f32),
            jax.ShapeDtypeStruct(struct_prev.shape, f32),
            jax.ShapeDtypeStruct(iterate.shape, f32),
        ),
        in_specs=[pl.BlockSpec(memory_space=pltpu.HBM)] * len(operands),
        out_specs=(vmem, vmem, vmem),
        scratch_shapes=[
            pltpu.VMEM((directions, depth + 2, width + 2 * PAD, span), f32),
            pltpu.VMEM((4, depth * width, span), f32),
            pltpu.VMEM((2, 5, width, span), f32),
            pltpu.VMEM((2, 5, width, span), f32),
            pltpu.VMEM((2, 5, depth, span), f32),
            pltpu.VMEM((2, 5, depth, span), f32),
            pltpu.VMEM((4, 8, span), f32),
            pltpu.VMEM((4, 8, span), f32),
            pltpu.VMEM((n, 3, SUB, BLOCK), f32),
            pltpu.VMEM((n, 3, SUB, BLOCK), f32),
            pltpu.VMEM((n, 3, SUB, BLOCK), f32),
            pltpu.VMEM((n, 3, SUB, BLOCK), f32),
            pltpu.VMEM((n, 8, BLOCK), f32),
            pltpu.VMEM((3 * BLOCK, 3 * nblocks), bf16),
            pltpu.VMEM((3, SUB, BLOCK), f32),
            pltpu.VMEM((12, elems), f32),
            pltpu.VMEM((12, elems), f32),
            pltpu.VMEM((3, SUB, BLOCK), f32),
            pltpu.VMEM((BLOCK, points), bf16),
            pltpu.VMEM((BLOCK, points), bf16),
            pltpu.VMEM((3, points), f32),
            pltpu.VMEM((3, points), f32),
            DMA((4, n)),
            DMA((4, n)),
            DMA((HALO_SLOTS,)),
            DMA((HALO_SLOTS,)),
            pltpu.VMEM((3, 8, points), f32),
            pltpu.VMEM((3, 8, points), f32),
            DMA((len(operands),)),
        ]
        + [pltpu.VMEM(x.shape, x.dtype) for x in operands],
        compiler_params=pltpu.CompilerParams(
            collective_id=0, has_side_effects=True, vmem_limit_bytes=63 * 2**20
        ),
    )(*operands)


def solution(mesh):
    lattice = P(None, ("groups", "slab"), "side", None)
    last = P(None, ("groups", "slab", "side"))
    one = P(("groups", "slab", "side"))
    deep = P(None, None, ("groups", "slab", "side"))
    return jax.shard_map(
        functools.partial(body, mesh.shape["slab"], mesh.shape["side"]),
        mesh=mesh,
        in_specs=(
            P(None, ("groups", "slab"), "side", None),
            P(("groups", "slab"), "side", None),
            one,
            P(("groups", "slab", "side"), None),
            one,
            last,
            last,
            last,
            last,
            one,
            last,
            deep,
            last,
            last,
            last,
            deep,
            deep,
        ),
        out_specs=(lattice, last, last),
        check_vma=False,
    )
```

```python
import functools

import jax
import jax.numpy as jnp
import numpy as np
from jax import lax
from jax.experimental import pallas as pl
from jax.experimental.pallas import tpu as pltpu
from jax.sharding import PartitionSpec as P

MESH = pl.DeviceIdType.MESH
BLOCK = 128
SUB = 8
PAD = 8
HALO_SLOTS = 8

velocities = np.array(
    [
        [0, 0, 0],
        [1, 0, 0],
        [-1, 0, 0],
        [0, 1, 0],
        [0, -1, 0],
        [0, 0, 1],
        [0, 0, -1],
        [1, 1, 0],
        [-1, -1, 0],
        [1, -1, 0],
        [-1, 1, 0],
        [1, 0, 1],
        [-1, 0, -1],
        [1, 0, -1],
        [-1, 0, 1],
        [0, 1, 1],
        [0, -1, -1],
        [0, 1, -1],
        [0, -1, 1],
    ]
)
lattice_weights = [1.0 / 3.0] + [1.0 / 18.0] * 6 + [1.0 / 36.0] * 12
relax_rate = 1.25
base_density = 19.0
support_scale = 0.1
f32, bf16 = jnp.float32, jnp.bfloat16

z_dirs = {s: [d for d in range(19) if velocities[d, 2] == s] for s in (1, -1)}
x_dirs = {s: [d for d in range(19) if velocities[d, 0] == s] for s in (1, -1)}
corners = [
    (d, int(velocities[d, 0]), int(velocities[d, 2]))
    for d in range(19)
    if velocities[d, 0] != 0 and velocities[d, 2] != 0
]


def pieces(x, count):
    out = []
    for _ in range(count - 1):
        part = x.astype(bf16)
        out.append(part)
        x = x - part.astype(f32)
    out.append(x.astype(bf16))
    return out


def stacked_pieces(x, count):
    out = []
    for _ in range(count - 1):
        part = x.astype(bf16).astype(f32)
        out.append(part)
        x = x - part
    out.append(x)
    return jnp.concatenate(out, axis=0).astype(bf16)


def mm(a, b):
    return jnp.dot(a, b, preferred_element_type=f32)


def mm_nt(a, b):
    return lax.dot_general(a, b, (((1,), (1,)), ((), ())), preferred_element_type=f32)


def rows_iota(rows, columns):
    return lax.broadcasted_iota(jnp.int32, (rows, columns), 0)


def onehot(index, rows):
    return jnp.where(rows_iota(rows, index.shape[1]) == index, 1.0, 0.0).astype(f32)


def fold_lanes(x):
    total = x[:, 0:128]
    for j in range(1, x.shape[1] // 128):
        total = total + x[:, j * 128 : (j + 1) * 128]
    return jnp.sum(total, axis=0, keepdims=True)


def kernel(
    n_slab,
    n_side,
    pop_in,
    mask_in,
    cell_in,
    owner_in,
    block_in,
    coords_in,
    normal_in,
    nodes_in,
    sprev_in,
    comp_in,
    enodes_in,
    stiff_in,
    iterate_in,
    rprev_in,
    iprev_in,
    rhist_in,
    ihist_in,
    out_pop,
    out_disp,
    out_iter,
    padded,
    fields,
    zsend,
    zrecv,
    xsend,
    xrecv,
    csend,
    crecv,
    nbuf,
    lsend,
    lrecv,
    dbuf,
    gbuf,
    wide,
    spb,
    dofs,
    force,
    stiffed,
    whi,
    wlo,
    tract,
    image,
    send_sem,
    recv_sem,
    hsend_sem,
    hrecv_sem,
    vcols,
    wcols,
    load_sem,
    groups,
    psend,
    precv,
    hbuf,
    pop,
    mask,
    cell,
    owner,
    block,
    coords,
    normal,
    nodes,
    sprev,
    comp,
    enodes,
    stiff,
    iterate,
    rprev,
    iprev,
    rhist,
    ihist,
):
    n = n_slab * n_side
    slab = lax.axis_index("slab")
    side = lax.axis_index("side")
    depth, width, span = pop.shape[1:]
    points = cell.shape[1]
    nblocks = n * SUB
    hist = rhist.shape[1]

    order = ("nodes", "sprev", "pop", "mask", "enodes", "stiff", "owner", "block", "coords")
    order += ("rhist", "ihist", "comp", "cell", "normal", "iterate", "rprev", "iprev")
    held = dict(
        pop=(pop_in, pop),
        mask=(mask_in, mask),
        cell=(cell_in, cell),
        owner=(owner_in, owner),
        block=(block_in, block),
        coords=(coords_in, coords),
        normal=(normal_in, normal),
        nodes=(nodes_in, nodes),
        sprev=(sprev_in, sprev),
        comp=(comp_in, comp),
        enodes=(enodes_in, enodes),
        stiff=(stiff_in, stiff),
        iterate=(iterate_in, iterate),
        rprev=(rprev_in, rprev),
        iprev=(iprev_in, iprev),
        rhist=(rhist_in, rhist),
        ihist=(ihist_in, ihist),
    )
    loads = {}
    for place, name in enumerate(order):
        loads[name] = pltpu.make_async_copy(*held[name], load_sem.at[place])
        loads[name].start()

    def ready(*names):
        for name in names:
            loads[name].wait()

    barrier = pltpu.get_barrier_semaphore()

    extent = {"slab": (n_slab, slab), "side": (n_side, side)}

    def partners(axis, act):
        size, mine = extent[axis]

        def one(o, carry):
            act((mine + o) % size)
            return carry

        if size <= 4:
            for o in range(1, size):
                one(o, 0)
        else:
            lax.fori_loop(1, size, one, 0)

    def greet(place):
        pl.semaphore_signal(barrier, inc=1, device_id=place, device_id_type=MESH)

    for axis in ("slab", "side"):
        partners(axis, lambda peer: greet({axis: peer}))
    for _, sx, sz in corners:
        greet({"slab": (slab + sz + n_slab) % n_slab, "side": (side + sx + n_side) % n_side})

    ready("nodes", "sprev")
    for hi in range(SUB):
        nbuf[side, slab, :, hi, :] = nodes[:, hi * 128 : (hi + 1) * 128]
        spb[:, hi, :] = sprev[:, hi * 128 : (hi + 1) * 128]
    pl.semaphore_wait(barrier, n_slab + n_side - 2 + len(corners))

    def transfer(stage, axis, peer, source, target, index):
        return pltpu.make_async_remote_copy(
            src_ref=source,
            dst_ref=target,
            send_sem=send_sem.at[stage, peer],
            recv_sem=recv_sem.at[stage, index],
            device_id={axis: peer},
            device_id_type=MESH,
        )

    def exchange(stage, axis, source, target):
        mine = extent[axis][1]
        partners(
            axis, lambda peer: transfer(stage, axis, peer, source(peer), target, mine).start()
        )

    def arrived(stage, axis, landing):
        partners(
            axis,
            lambda peer: transfer(
                stage, axis, peer, landing(peer), landing(peer), peer
            ).wait_recv(),
        )

    def departed(stage, axis, source):
        partners(
            axis,
            lambda peer: transfer(
                stage, axis, peer, source(peer), source(peer), peer
            ).wait_send(),
        )

    exchange(0, "slab", lambda peer: nbuf.at[side, slab], nbuf.at[side, slab])

    ready("pop", "mask")
    chunks = width // 8

    def collide(z, i):
        x = pl.multiple_of(i * 8, 8)
        xp = pl.multiple_of(i * 8 + PAD, 8)
        f = [pop[d, z, pl.ds(x, 8), :] for d in range(19)]
        solid = mask[z, pl.ds(x, 8), :] == 1
        density = f[0]
        mom = [None, None, None]
        for d in range(1, 19, 2):
            density = density + (f[d] + f[d + 1])
            diff = f[d] - f[d + 1]
            for axis in range(3):
                c = int(velocities[d, axis])
                if c:
                    if mom[axis] is None:
                        mom[axis] = diff if c > 0 else -diff
                    else:
                        mom[axis] = mom[axis] + diff if c > 0 else mom[axis] - diff
        inv = 1.0 / density
        u = [m * inv for m in mom]
        base = 1.0 - 1.5 * (u[0] * u[0] + u[1] * u[1] + u[2] * u[2])
        keep = 1.0 - relax_rate
        weighted = density * (relax_rate * lattice_weights[0])
        padded[0, z + 1, pl.ds(xp, 8), :] = jnp.where(solid, f[0], keep * f[0] + weighted * base)
        scaled = {w: density * (relax_rate * w) for w in (1.0 / 18.0, 1.0 / 36.0)}
        for d in range(1, 19, 2):
            project = None
            for axis in range(3):
                c = int(velocities[d, axis])
                if c:
                    if project is None:
                        project = u[axis] if c > 0 else -u[axis]
                    else:
                        project = project + u[axis] if c > 0 else project - u[axis]
            w = scaled[lattice_weights[d]]
            even = w * (base + 4.5 * project * project)
            odd = w * (3.0 * project)
            padded[d, z + 1, pl.ds(xp, 8), :] = jnp.where(
                solid, f[d + 1], keep * f[d] + (even + odd)
            )
            padded[d + 1, z + 1, pl.ds(xp, 8), :] = jnp.where(
                solid, f[d], keep * f[d + 1] + (even - odd)
            )

    def outer_planes(i, carry):
        collide((i // chunks) * (depth - 1), i % chunks)
        return carry

    def inner_planes(i, carry):
        collide(1 + i // chunks, i % chunks)
        return carry

    halo_copies = []

    def pass_halo(source, target, index, place):
        copy = pltpu.make_async_remote_copy(
            src_ref=source,
            dst_ref=target,
            send_sem=hsend_sem.at[index],
            recv_sem=hrecv_sem.at[index],
            device_id=place,
            device_id_type=MESH,
        )
        copy.start()
        halo_copies.append(copy)

    lax.fori_loop(0, 2 * chunks, outer_planes, 0)
    for slot, s in enumerate((1, -1)):
        plane = depth if s > 0 else 1
        for j, d in enumerate(z_dirs[s]):
            zsend[slot, j] = padded[d, plane, PAD : PAD + width, :]
        place = {"slab": (slab + s + n_slab) % n_slab}
        pass_halo(zsend.at[slot], zrecv.at[slot], slot, place)
    lax.fori_loop(0, (depth - 2) * chunks, inner_planes, 0)
    for slot, s in enumerate((1, -1)):
        row = PAD + width - 1 if s > 0 else PAD
        for j, d in enumerate(x_dirs[s]):
            for z in range(depth):
                xsend[slot, j, z : z + 1, :] = padded[d, 1 + z, row : row + 1, :]
        place = {"side": (side + s + n_side) % n_side}
        pass_halo(xsend.at[slot], xrecv.at[slot], 2 + slot, place)
    for slot, (d, sx, sz) in enumerate(corners):
        plane = depth if sz > 0 else 1
        row = PAD + width - 1 if sx > 0 else PAD
        csend[slot] = jnp.broadcast_to(padded[d, plane, row : row + 1, :], (8, span))
        place = {
            "slab": (slab + sz + n_slab) % n_slab,
            "side": (side + sx + n_side) % n_side,
        }
        pass_halo(csend.at[slot], crecv.at[slot], 4 + slot, place)
    arrived(0, "slab", lambda peer: nbuf.at[side, peer])
    exchange(1, "side", lambda peer: nbuf.at[side], nbuf.at[side])

    ready("enodes", "stiff")
    elems = enodes.shape[1]
    prev_pieces = stacked_pieces(spb[...].reshape(3 * SUB, 128), 3)
    rows = 3 * SUB
    for c in range(4):
        ids = enodes[c : c + 1, :]
        low = onehot(ids & 127, 128).astype(bf16)
        high = rows_iota(SUB, elems) == (ids >> 7)
        got = mm(prev_pieces, low)
        got = got[0:rows] + got[rows : 2 * rows] + got[2 * rows : 3 * rows]
        for k in range(3):
            part = jnp.where(high, got[k * SUB : (k + 1) * SUB], 0.0)
            dofs[3 * c + k : 3 * c + k + 1, :] = jnp.sum(part, axis=0, keepdims=True)
    local = dofs[...]
    for i in range(12):
        force[i : i + 1, :] = jnp.sum(stiff[i] * local, axis=0, keepdims=True)
    total = jnp.zeros((3 * rows, 128), f32)
    for c in range(4):
        ids = enodes[c : c + 1, :]
        low = onehot(ids & 127, 128).astype(bf16)
        high = rows_iota(SUB, elems) == (ids >> 7)
        spread = [jnp.where(high, force[3 * c + k : 3 * c + k + 1, :], 0.0) for k in range(3)]
        total = total + mm_nt(stacked_pieces(jnp.concatenate(spread, axis=0), 3), low)
    total = total[0:rows] + total[rows : 2 * rows] + total[2 * rows : 3 * rows]
    stiffed[...] = total.reshape(3, SUB, 128)

    ready("rhist", "ihist")
    for k in range(3):
        vcols[k] = jnp.zeros(vcols.shape[1:], f32)
        wcols[k] = jnp.zeros(wcols.shape[1:], f32)
        vcols[k, 1 : 1 + hist, :] = rhist[k]
        wcols[k, 1 : 1 + hist, :] = ihist[k]

    ready("owner", "block", "coords")
    arrived(1, "side", lambda peer: nbuf.at[peer])
    holder = owner[...]
    groups[...] = ((holder % n_side) * n_slab + holder // n_side) * SUB + block[...]
    step = 512 if nblocks <= 128 else 128
    node_pieces = []
    for k in range(3):
        turned = nbuf[:, :, k].reshape(nblocks, BLOCK).T
        node_pieces.append(jnp.concatenate(pieces(turned, 3), axis=1))
    wide[...] = jnp.concatenate(node_pieces, axis=0)

    def group_of(at):
        return groups[:, pl.ds(at, step)]

    def weigh(i, carry):
        at = pl.multiple_of(i * step, step)
        hot = onehot(group_of(at), nblocks).astype(bf16)
        support = mm(wide[...], jnp.concatenate([hot, hot, hot], axis=0))
        distance = None
        for k in range(3):
            offset = support[k * BLOCK : (k + 1) * BLOCK] - coords[k : k + 1, pl.ds(at, step)]
            square = offset * offset
            distance = square if distance is None else distance + square
        phi = 1.0 / (1.0 + distance * (1.0 / support_scale))
        weight = phi * (1.0 / jnp.sum(phi, axis=0, keepdims=True))
        upper, lower = pieces(weight, 2)
        whi[:, pl.ds(at, step)] = upper
        wlo[:, pl.ds(at, step)] = lower
        return carry

    lax.fori_loop(0, points // step, weigh, 0)

    for copy in halo_copies:
        copy.wait_recv()
    for slot, s in enumerate((1, -1)):
        plane = 0 if s > 0 else depth + 1
        for j, d in enumerate(z_dirs[s]):
            padded[d, plane, PAD : PAD + width, :] = zrecv[slot, j]
    for slot, s in enumerate((1, -1)):
        row = PAD - 1 if s > 0 else PAD + width
        for j, d in enumerate(x_dirs[s]):
            for z in range(depth):
                padded[d, 1 + z, row : row + 1, :] = xrecv[slot, j, z : z + 1, :]
    for slot, (d, sx, sz) in enumerate(corners):
        plane = 0 if sz > 0 else depth + 1
        row = PAD - 1 if sx > 0 else PAD + width
        padded[d, plane, row : row + 1, :] = crecv[slot, 0:1, :]

    def stream(z, carry):
        for x in range(0, width, 16):
            density = None
            mom = [None, None, None]
            for d in range(19):
                cx, cy, cz = (int(v) for v in velocities[d])
                piece = padded[d, z + 1 - cz, PAD + x - cx : PAD + x - cx + 16, :]
                if cy:
                    piece = pltpu.roll(piece, cy % span, 1)
                out_pop[d, z, x : x + 16, :] = piece
                density = piece if density is None else density + piece
                for axis, c in enumerate((cx, cy, cz)):
                    if c:
                        if mom[axis] is None:
                            mom[axis] = piece if c > 0 else -piece
                        else:
                            mom[axis] = mom[axis] + piece if c > 0 else mom[axis] - piece
            where = pl.ds(pl.multiple_of(z * width + x, 16), 16)
            fields[0, where, :] = (density - base_density) * (1.0 / 3.0)
            for axis in range(3):
                fields[1 + axis, where, :] = mom[axis]
        return carry

    lax.fori_loop(0, depth, stream, 0)

    ready("cell", "normal")
    cells = depth * width
    turned = jnp.concatenate([fields[k].T for k in range(4)], axis=0)
    turned_hi, turned_lo = pieces(turned, 2)
    tstep = 512

    def sample(i, carry):
        at = pl.multiple_of(i * tstep, tstep)
        ids = cell[:, pl.ds(at, tstep)]
        hot = onehot(ids // span, cells).astype(bf16)
        picked = mm(turned_hi, hot) + mm(turned_lo, hot)
        chosen = rows_iota(span, tstep) == (ids % span)
        got = []
        for k in range(4):
            part = jnp.where(chosen, picked[k * span : (k + 1) * span], 0.0)
            got.append(jnp.sum(part, axis=0, keepdims=True))
        for k in range(3):
            tract[k : k + 1, pl.ds(at, tstep)] = (
                got[0] * normal[k : k + 1, pl.ds(at, tstep)] + got[1 + k]
            )
        return carry

    lax.fori_loop(0, points // tstep, sample, 0)

    def gather_load(i, total):
        at = pl.multiple_of(i * step, step)
        chosen = rows_iota(nblocks, step) == group_of(at)
        spread = [jnp.where(chosen, tract[k : k + 1, pl.ds(at, step)], 0.0) for k in range(3)]
        upper, lower = pieces(jnp.concatenate(spread, axis=0), 2)
        first, second = whi[:, pl.ds(at, step)], wlo[:, pl.ds(at, step)]
        return total + (mm_nt(upper, first) + (mm_nt(lower, first) + mm_nt(upper, second)))

    load = lax.fori_loop(
        0, points // step, gather_load, jnp.zeros((3 * nblocks, BLOCK), f32)
    )
    for k in range(3):
        lsend[:, :, k] = load[k * nblocks : (k + 1) * nblocks].reshape(
            n_side, n_slab, SUB, BLOCK
        )
    exchange(2, "side", lambda peer: lsend.at[peer], lrecv.at[side])
    lrecv[side] = lsend[side]
    ready("comp")
    arrived(2, "side", lambda peer: lrecv.at[peer])
    psend[...] = jnp.sum(lrecv[...], axis=0)
    exchange(3, "slab", lambda peer: psend.at[peer], precv.at[slab])
    precv[slab] = psend[slab]
    arrived(3, "slab", lambda peer: precv.at[peer])
    load = jnp.sum(precv[...], axis=0)
    disp = spb[...] + comp[...][None] * (load - stiffed[...])
    dbuf[side, slab] = disp
    exchange(4, "slab", lambda peer: dbuf.at[side, slab], dbuf.at[side, slab])
    for hi in range(SUB):
        out_disp[:, hi * 128 : (hi + 1) * 128] = dbuf[side, slab, :, hi, :]
    arrived(4, "slab", lambda peer: dbuf.at[side, peer])
    exchange(5, "side", lambda peer: dbuf.at[side], dbuf.at[side])
    arrived(5, "side", lambda peer: dbuf.at[peer])

    field = jnp.concatenate([dbuf[:, :, k].reshape(nblocks, BLOCK) for k in range(3)], axis=0)
    field_hi, field_lo = pieces(field, 2)

    def map_back(i, carry):
        at = pl.multiple_of(i * step, step)
        first, second = whi[:, pl.ds(at, step)], wlo[:, pl.ds(at, step)]
        mapped = mm(field_hi, first) + (mm(field_lo, first) + mm(field_hi, second))
        chosen = rows_iota(nblocks, step) == group_of(at)
        for k in range(3):
            part = jnp.where(chosen, mapped[k * nblocks : (k + 1) * nblocks], 0.0)
            image[k : k + 1, pl.ds(at, step)] = jnp.sum(part, axis=0, keepdims=True)
        return carry

    lax.fori_loop(0, points // step, map_back, 0)

    ready("iterate", "rprev", "iprev")
    gram = None
    for k in range(3):
        now = image[k : k + 1, :]
        resid = now - iterate[k : k + 1, :]
        vcols[k, 0:1, :] = resid - rprev[k : k + 1, :]
        vcols[k, 1 + hist : 2 + hist, :] = resid
        wcols[k, 0:1, :] = now - iprev[k : k + 1, :]
        parts = stacked_pieces(vcols[k], 3)
        term = mm_nt(parts, parts)
        gram = term if gram is None else gram + term
    gram = gram[0:8] + gram[8:16] + gram[16:24]
    gram = gram[:, 0:8] + gram[:, 8:16] + gram[:, 16:24]
    gbuf[side] = jnp.concatenate([gram, jnp.zeros((8, BLOCK - 8), f32)], axis=1)
    exchange(6, "side", lambda peer: gbuf.at[side], gbuf.at[side])
    arrived(6, "side", lambda peer: gbuf.at[peer])
    hbuf[slab] = jnp.sum(gbuf[...], axis=0)
    exchange(7, "slab", lambda peer: hbuf.at[slab], hbuf.at[slab])
    arrived(7, "slab", lambda peer: hbuf.at[peer])
    sums = jnp.sum(hbuf[...], axis=0)
    size = hist + 1

    matrix = [[sums[i : i + 1, j : j + 1] for j in range(size)] for i in range(size)]
    rhs = [-sums[i : i + 1, size : size + 1] for i in range(size)]
    for pivot in range(size):
        scale = 1.0 / matrix[pivot][pivot]
        row_vals = [v * scale for v in matrix[pivot]]
        value = rhs[pivot] * scale
        for i in range(size):
            if i != pivot:
                factor = matrix[i][pivot]
                matrix[i] = [matrix[i][j] - factor * row_vals[j] for j in range(size)]
                rhs[i] = rhs[i] - factor * value
        matrix[pivot], rhs[pivot] = row_vals, value
    coeffs = jnp.concatenate(rhs + [jnp.zeros((8 - size, 1), f32)], axis=0)
    for k in range(3):
        change = jnp.sum(wcols[k] * coeffs, axis=0, keepdims=True)
        out_iter[k : k + 1, :] = image[k : k + 1, :] + change

    for copy in halo_copies:
        copy.wait_send()
    departed(0, "slab", lambda peer: nbuf.at[side, slab])
    departed(1, "side", lambda peer: nbuf.at[side])
    departed(2, "side", lambda peer: lsend.at[peer])
    departed(3, "slab", lambda peer: psend.at[peer])
    departed(4, "slab", lambda peer: dbuf.at[side, slab])
    departed(5, "side", lambda peer: dbuf.at[side])
    departed(6, "side", lambda peer: gbuf.at[side])
    departed(7, "slab", lambda peer: hbuf.at[slab])


def body(n_slab, n_side, *args):
    (
        populations,
        solid_mask,
        point_cell,
        point_owner,
        point_block,
        point_coords,
        point_normal,
        node_coords,
        struct_prev,
        compliance,
        elem_nodes,
        elem_stiff,
        iterate,
        resid_prev,
        image_prev,
        resid_history,
        image_history,
    ) = args
    n = n_slab * n_side
    directions, depth, width, span = populations.shape
    points = point_cell.shape[0]
    elems = elem_nodes.shape[1]
    nblocks = n * SUB
    vmem = pl.BlockSpec(memory_space=pltpu.VMEM)
    DMA = pltpu.SemaphoreType.DMA
    operands = (
        populations,
        solid_mask,
        point_cell.reshape(1, points),
        point_owner.reshape(1, points),
        point_block.reshape(1, points),
        point_coords,
        point_normal,
        node_coords,
        struct_prev,
        compliance.reshape(SUB, BLOCK),
        elem_nodes,
        elem_stiff,
        iterate,
        resid_prev,
        image_prev,
        resid_history.transpose(1, 0, 2),
        image_history.transpose(1, 0, 2),
    )
    return pl.pallas_call(
        functools.partial(kernel, n_slab, n_side),
        out_shape=(
            jax.ShapeDtypeStruct(populations.shape, f32),
            jax.ShapeDtypeStruct(struct_prev.shape, f32),
            jax.ShapeDtypeStruct(iterate.shape, f32),
        ),
        in_specs=[pl.BlockSpec(memory_space=pltpu.HBM)] * len(operands),
        out_specs=(vmem, vmem, vmem),
        scratch_shapes=[
            pltpu.VMEM((directions, depth + 2, width + 2 * PAD, span), f32),
            pltpu.VMEM((4, depth * width, span), f32),
            pltpu.VMEM((2, 5, width, span), f32),
            pltpu.VMEM((2, 5, width, span), f32),
            pltpu.VMEM((2, 5, depth, span), f32),
            pltpu.VMEM((2, 5, depth, span), f32),
            pltpu.VMEM((4, 8, span), f32),
            pltpu.VMEM((4, 8, span), f32),
            pltpu.VMEM((n_side, n_slab, 3, SUB, BLOCK), f32),
            pltpu.VMEM((n_side, n_slab, 3, SUB, BLOCK), f32),
            pltpu.VMEM((n_side, n_slab, 3, SUB, BLOCK), f32),
            pltpu.VMEM((n_side, n_slab, 3, SUB, BLOCK), f32),
            pltpu.VMEM((n_side, 8, BLOCK), f32),
            pltpu.VMEM((3 * BLOCK, 3 * nblocks), bf16),
            pltpu.VMEM((3, SUB, BLOCK), f32),
            pltpu.VMEM((12, elems), f32),
            pltpu.VMEM((12, elems), f32),
            pltpu.VMEM((3, SUB, BLOCK), f32),
            pltpu.VMEM((BLOCK, points), bf16),
            pltpu.VMEM((BLOCK, points), bf16),
            pltpu.VMEM((3, points), f32),
            pltpu.VMEM((3, points), f32),
            DMA((8, max(n_slab, n_side))),
            DMA((8, max(n_slab, n_side))),
            DMA((HALO_SLOTS,)),
            DMA((HALO_SLOTS,)),
            pltpu.VMEM((3, 8, points), f32),
            pltpu.VMEM((3, 8, points), f32),
            DMA((len(operands),)),
            pltpu.VMEM((1, points), jnp.int32),
            pltpu.VMEM((n_slab, 3, SUB, BLOCK), f32),
            pltpu.VMEM((n_slab, 3, SUB, BLOCK), f32),
            pltpu.VMEM((n_slab, 8, BLOCK), f32),
        ]
        + [pltpu.VMEM(x.shape, x.dtype) for x in operands],
        compiler_params=pltpu.CompilerParams(
            collective_id=0, has_side_effects=True, vmem_limit_bytes=63 * 2**20
        ),
    )(*operands)


def solution(mesh):
    lattice = P(None, ("groups", "slab"), "side", None)
    last = P(None, ("groups", "slab", "side"))
    one = P(("groups", "slab", "side"))
    deep = P(None, None, ("groups", "slab", "side"))
    return jax.shard_map(
        functools.partial(body, mesh.shape["slab"], mesh.shape["side"]),
        mesh=mesh,
        in_specs=(
            P(None, ("groups", "slab"), "side", None),
            P(("groups", "slab"), "side", None),
            one,
            P(("groups", "slab", "side"), None),
            one,
            last,
            last,
            last,
            last,
            one,
            last,
            deep,
            last,
            last,
            last,
            deep,
            deep,
        ),
        out_specs=(lattice, last, last),
        check_vma=False,
    )
```

```python
import functools

import jax
import jax.numpy as jnp
import numpy as np
from jax import lax
from jax.experimental import pallas as pl
from jax.experimental.pallas import tpu as pltpu
from jax.sharding import PartitionSpec as P

MESH = pl.DeviceIdType.MESH
BLOCK = 128
SUB = 8
PAD = 8
HALO_SLOTS = 8

velocities = np.array(
    [
        [0, 0, 0],
        [1, 0, 0],
        [-1, 0, 0],
        [0, 1, 0],
        [0, -1, 0],
        [0, 0, 1],
        [0, 0, -1],
        [1, 1, 0],
        [-1, -1, 0],
        [1, -1, 0],
        [-1, 1, 0],
        [1, 0, 1],
        [-1, 0, -1],
        [1, 0, -1],
        [-1, 0, 1],
        [0, 1, 1],
        [0, -1, -1],
        [0, 1, -1],
        [0, -1, 1],
    ]
)
lattice_weights = [1.0 / 3.0] + [1.0 / 18.0] * 6 + [1.0 / 36.0] * 12
relax_rate = 1.25
base_density = 19.0
support_scale = 0.1
f32, bf16 = jnp.float32, jnp.bfloat16

z_dirs = {s: [d for d in range(19) if velocities[d, 2] == s] for s in (1, -1)}
x_dirs = {s: [d for d in range(19) if velocities[d, 0] == s] for s in (1, -1)}
corners = [
    (d, int(velocities[d, 0]), int(velocities[d, 2]))
    for d in range(19)
    if velocities[d, 0] != 0 and velocities[d, 2] != 0
]


def pieces(x, count):
    out = []
    for _ in range(count - 1):
        part = x.astype(bf16)
        out.append(part)
        x = x - part.astype(f32)
    out.append(x.astype(bf16))
    return out


def stacked_pieces(x, count):
    out = []
    for _ in range(count - 1):
        part = x.astype(bf16).astype(f32)
        out.append(part)
        x = x - part
    out.append(x)
    return jnp.concatenate(out, axis=0).astype(bf16)


def mm(a, b):
    return jnp.dot(a, b, preferred_element_type=f32)


def mm_nt(a, b):
    return lax.dot_general(a, b, (((1,), (1,)), ((), ())), preferred_element_type=f32)


def rows_iota(rows, columns):
    return lax.broadcasted_iota(jnp.int32, (rows, columns), 0)


def onehot(index, rows):
    return jnp.where(rows_iota(rows, index.shape[1]) == index, 1.0, 0.0).astype(f32)


def fold_lanes(x):
    total = x[:, 0:128]
    for j in range(1, x.shape[1] // 128):
        total = total + x[:, j * 128 : (j + 1) * 128]
    return jnp.sum(total, axis=0, keepdims=True)


def kernel(
    n_slab,
    n_side,
    pop_in,
    mask_in,
    cell_in,
    owner_in,
    block_in,
    coords_in,
    normal_in,
    nodes_in,
    sprev_in,
    comp_in,
    enodes_in,
    stiff_in,
    iterate_in,
    rprev_in,
    iprev_in,
    rhist_in,
    ihist_in,
    out_pop,
    out_disp,
    out_iter,
    padded,
    fields,
    zsend,
    zrecv,
    xsend,
    xrecv,
    csend,
    crecv,
    nbuf,
    lsend,
    lrecv,
    dbuf,
    gbuf,
    wide,
    spb,
    dofs,
    force,
    stiffed,
    whi,
    wlo,
    tract,
    image,
    send_sem,
    recv_sem,
    hsend_sem,
    hrecv_sem,
    vcols,
    wcols,
    load_sem,
    groups,
    psend,
    precv,
    hbuf,
    moved,
    out_sem,
    pop,
    mask,
    cell,
    owner,
    block,
    coords,
    normal,
    nodes,
    sprev,
    comp,
    enodes,
    stiff,
    iterate,
    rprev,
    iprev,
    rhist,
    ihist,
):
    n = n_slab * n_side
    slab = lax.axis_index("slab")
    side = lax.axis_index("side")
    depth, width, span = pop.shape[1:]
    points = cell.shape[1]
    nblocks = n * SUB
    hist = rhist.shape[1]

    order = ("nodes", "sprev", "pop", "mask", "enodes", "stiff", "owner", "block", "coords")
    order += ("rhist", "ihist", "comp", "cell", "normal", "iterate", "rprev", "iprev")
    held = dict(
        pop=(pop_in, pop),
        mask=(mask_in, mask),
        cell=(cell_in, cell),
        owner=(owner_in, owner),
        block=(block_in, block),
        coords=(coords_in, coords),
        normal=(normal_in, normal),
        nodes=(nodes_in, nodes),
        sprev=(sprev_in, sprev),
        comp=(comp_in, comp),
        enodes=(enodes_in, enodes),
        stiff=(stiff_in, stiff),
        iterate=(iterate_in, iterate),
        rprev=(rprev_in, rprev),
        iprev=(iprev_in, iprev),
        rhist=(rhist_in, rhist),
        ihist=(ihist_in, ihist),
    )
    loads = {}
    for place, name in enumerate(order):
        loads[name] = pltpu.make_async_copy(*held[name], load_sem.at[place])
        loads[name].start()

    def ready(*names):
        for name in names:
            loads[name].wait()

    barrier = pltpu.get_barrier_semaphore()

    extent = {"slab": (n_slab, slab), "side": (n_side, side)}

    def partners(axis, act):
        size, mine = extent[axis]

        def one(o, carry):
            act((mine + o) % size)
            return carry

        if size <= 4:
            for o in range(1, size):
                one(o, 0)
        else:
            lax.fori_loop(1, size, one, 0)

    def greet(place):
        pl.semaphore_signal(barrier, inc=1, device_id=place, device_id_type=MESH)

    for axis in ("slab", "side"):
        partners(axis, lambda peer: greet({axis: peer}))
    for _, sx, sz in corners:
        greet({"slab": (slab + sz + n_slab) % n_slab, "side": (side + sx + n_side) % n_side})

    ready("nodes", "sprev")
    for hi in range(SUB):
        nbuf[side, slab, :, hi, :] = nodes[:, hi * 128 : (hi + 1) * 128]
        spb[:, hi, :] = sprev[:, hi * 128 : (hi + 1) * 128]
    pl.semaphore_wait(barrier, n_slab + n_side - 2 + len(corners))

    def transfer(stage, axis, peer, source, target, index):
        return pltpu.make_async_remote_copy(
            src_ref=source,
            dst_ref=target,
            send_sem=send_sem.at[stage, peer],
            recv_sem=recv_sem.at[stage, index],
            device_id={axis: peer},
            device_id_type=MESH,
        )

    def exchange(stage, axis, source, target):
        mine = extent[axis][1]
        partners(
            axis, lambda peer: transfer(stage, axis, peer, source(peer), target, mine).start()
        )

    def arrived(stage, axis, landing):
        partners(
            axis,
            lambda peer: transfer(
                stage, axis, peer, landing(peer), landing(peer), peer
            ).wait_recv(),
        )

    def departed(stage, axis, source):
        partners(
            axis,
            lambda peer: transfer(
                stage, axis, peer, source(peer), source(peer), peer
            ).wait_send(),
        )

    exchange(0, "slab", lambda peer: nbuf.at[side, slab], nbuf.at[side, slab])

    ready("pop", "mask")
    chunks = width // 8

    def collide(z, i):
        x = pl.multiple_of(i * 8, 8)
        xp = pl.multiple_of(i * 8 + PAD, 8)
        f = [pop[d, z, pl.ds(x, 8), :] for d in range(19)]
        solid = mask[z, pl.ds(x, 8), :] == 1
        density = f[0]
        mom = [None, None, None]
        for d in range(1, 19, 2):
            density = density + (f[d] + f[d + 1])
            diff = f[d] - f[d + 1]
            for axis in range(3):
                c = int(velocities[d, axis])
                if c:
                    if mom[axis] is None:
                        mom[axis] = diff if c > 0 else -diff
                    else:
                        mom[axis] = mom[axis] + diff if c > 0 else mom[axis] - diff
        inv = 1.0 / density
        u = [m * inv for m in mom]
        base = 1.0 - 1.5 * (u[0] * u[0] + u[1] * u[1] + u[2] * u[2])
        keep = 1.0 - relax_rate
        weighted = density * (relax_rate * lattice_weights[0])
        padded[0, z + 1, pl.ds(xp, 8), :] = jnp.where(solid, f[0], keep * f[0] + weighted * base)
        scaled = {w: density * (relax_rate * w) for w in (1.0 / 18.0, 1.0 / 36.0)}
        for d in range(1, 19, 2):
            project = None
            for axis in range(3):
                c = int(velocities[d, axis])
                if c:
                    if project is None:
                        project = u[axis] if c > 0 else -u[axis]
                    else:
                        project = project + u[axis] if c > 0 else project - u[axis]
            w = scaled[lattice_weights[d]]
            even = w * (base + 4.5 * project * project)
            odd = w * (3.0 * project)
            padded[d, z + 1, pl.ds(xp, 8), :] = jnp.where(
                solid, f[d + 1], keep * f[d] + (even + odd)
            )
            padded[d + 1, z + 1, pl.ds(xp, 8), :] = jnp.where(
                solid, f[d], keep * f[d + 1] + (even - odd)
            )

    def outer_planes(i, carry):
        collide((i // chunks) * (depth - 1), i % chunks)
        return carry

    def inner_planes(i, carry):
        collide(1 + i // chunks, i % chunks)
        return carry

    halo_copies = []

    def pass_halo(source, target, index, place):
        copy = pltpu.make_async_remote_copy(
            src_ref=source,
            dst_ref=target,
            send_sem=hsend_sem.at[index],
            recv_sem=hrecv_sem.at[index],
            device_id=place,
            device_id_type=MESH,
        )
        copy.start()
        halo_copies.append(copy)

    lax.fori_loop(0, 2 * chunks, outer_planes, 0)
    for slot, s in enumerate((1, -1)):
        plane = depth if s > 0 else 1
        for j, d in enumerate(z_dirs[s]):
            zsend[slot, j] = padded[d, plane, PAD : PAD + width, :]
        place = {"slab": (slab + s + n_slab) % n_slab}
        pass_halo(zsend.at[slot], zrecv.at[slot], slot, place)
    lax.fori_loop(0, (depth - 2) * chunks, inner_planes, 0)
    for slot, s in enumerate((1, -1)):
        row = PAD + width - 1 if s > 0 else PAD
        for j, d in enumerate(x_dirs[s]):
            for z in range(depth):
                xsend[slot, j, z : z + 1, :] = padded[d, 1 + z, row : row + 1, :]
        place = {"side": (side + s + n_side) % n_side}
        pass_halo(xsend.at[slot], xrecv.at[slot], 2 + slot, place)
    for slot, (d, sx, sz) in enumerate(corners):
        plane = depth if sz > 0 else 1
        row = PAD + width - 1 if sx > 0 else PAD
        csend[slot] = jnp.broadcast_to(padded[d, plane, row : row + 1, :], (8, span))
        place = {
            "slab": (slab + sz + n_slab) % n_slab,
            "side": (side + sx + n_side) % n_side,
        }
        pass_halo(csend.at[slot], crecv.at[slot], 4 + slot, place)
    arrived(0, "slab", lambda peer: nbuf.at[side, peer])
    exchange(1, "side", lambda peer: nbuf.at[side], nbuf.at[side])

    ready("enodes", "stiff")
    elems = enodes.shape[1]
    prev_pieces = stacked_pieces(spb[...].reshape(3 * SUB, 128), 3)
    rows = 3 * SUB
    for c in range(4):
        ids = enodes[c : c + 1, :]
        low = onehot(ids & 127, 128).astype(bf16)
        high = rows_iota(SUB, elems) == (ids >> 7)
        got = mm(prev_pieces, low)
        got = got[0:rows] + got[rows : 2 * rows] + got[2 * rows : 3 * rows]
        for k in range(3):
            part = jnp.where(high, got[k * SUB : (k + 1) * SUB], 0.0)
            dofs[3 * c + k : 3 * c + k + 1, :] = jnp.sum(part, axis=0, keepdims=True)
    local = dofs[...]
    for i in range(12):
        force[i : i + 1, :] = jnp.sum(stiff[i] * local, axis=0, keepdims=True)
    total = jnp.zeros((3 * rows, 128), f32)
    for c in range(4):
        ids = enodes[c : c + 1, :]
        low = onehot(ids & 127, 128).astype(bf16)
        high = rows_iota(SUB, elems) == (ids >> 7)
        spread = [jnp.where(high, force[3 * c + k : 3 * c + k + 1, :], 0.0) for k in range(3)]
        total = total + mm_nt(stacked_pieces(jnp.concatenate(spread, axis=0), 3), low)
    total = total[0:rows] + total[rows : 2 * rows] + total[2 * rows : 3 * rows]
    stiffed[...] = total.reshape(3, SUB, 128)

    ready("rhist", "ihist")
    for k in range(3):
        vcols[k] = jnp.zeros(vcols.shape[1:], f32)
        wcols[k] = jnp.zeros(wcols.shape[1:], f32)
        vcols[k, 1 : 1 + hist, :] = rhist[k]
        wcols[k, 1 : 1 + hist, :] = ihist[k]

    ready("owner", "block", "coords")
    arrived(1, "side", lambda peer: nbuf.at[peer])
    holder = owner[...]
    groups[...] = ((holder % n_side) * n_slab + holder // n_side) * SUB + block[...]
    step = 512 if nblocks <= 128 else 128
    node_pieces = []
    for k in range(3):
        turned = nbuf[:, :, k].reshape(nblocks, BLOCK).T
        node_pieces.append(jnp.concatenate(pieces(turned, 3), axis=1))
    wide[...] = jnp.concatenate(node_pieces, axis=0)

    def group_of(at):
        return groups[:, pl.ds(at, step)]

    def weigh(i, carry):
        at = pl.multiple_of(i * step, step)
        hot = onehot(group_of(at), nblocks).astype(bf16)
        support = mm(wide[...], jnp.concatenate([hot, hot, hot], axis=0))
        distance = None
        for k in range(3):
            offset = support[k * BLOCK : (k + 1) * BLOCK] - coords[k : k + 1, pl.ds(at, step)]
            square = offset * offset
            distance = square if distance is None else distance + square
        phi = 1.0 / (1.0 + distance * (1.0 / support_scale))
        weight = phi * (1.0 / jnp.sum(phi, axis=0, keepdims=True))
        upper, lower = pieces(weight, 2)
        whi[:, pl.ds(at, step)] = upper
        wlo[:, pl.ds(at, step)] = lower
        return carry

    lax.fori_loop(0, points // step, weigh, 0)

    for copy in halo_copies:
        copy.wait_recv()
    for slot, s in enumerate((1, -1)):
        plane = 0 if s > 0 else depth + 1
        for j, d in enumerate(z_dirs[s]):
            padded[d, plane, PAD : PAD + width, :] = zrecv[slot, j]
    for slot, s in enumerate((1, -1)):
        row = PAD - 1 if s > 0 else PAD + width
        for j, d in enumerate(x_dirs[s]):
            for z in range(depth):
                padded[d, 1 + z, row : row + 1, :] = xrecv[slot, j, z : z + 1, :]
    for slot, (d, sx, sz) in enumerate(corners):
        plane = 0 if sz > 0 else depth + 1
        row = PAD - 1 if sx > 0 else PAD + width
        padded[d, plane, row : row + 1, :] = crecv[slot, 0:1, :]

    def stream(z, carry):
        for x in range(0, width, 16):
            density = None
            mom = [None, None, None]
            for d in range(19):
                cx, cy, cz = (int(v) for v in velocities[d])
                piece = padded[d, z + 1 - cz, PAD + x - cx : PAD + x - cx + 16, :]
                if cy:
                    piece = pltpu.roll(piece, cy % span, 1)
                moved[d, z, x : x + 16, :] = piece
                density = piece if density is None else density + piece
                for axis, c in enumerate((cx, cy, cz)):
                    if c:
                        if mom[axis] is None:
                            mom[axis] = piece if c > 0 else -piece
                        else:
                            mom[axis] = mom[axis] + piece if c > 0 else mom[axis] - piece
            where = pl.ds(pl.multiple_of(z * width + x, 16), 16)
            fields[0, where, :] = (density - base_density) * (1.0 / 3.0)
            for axis in range(3):
                fields[1 + axis, where, :] = mom[axis]
        return carry

    lax.fori_loop(0, depth, stream, 0)
    leaving = pltpu.make_async_copy(moved, out_pop, out_sem)
    leaving.start()

    ready("cell", "normal")
    cells = depth * width
    turned = jnp.concatenate([fields[k].T for k in range(4)], axis=0)
    turned_hi, turned_lo = pieces(turned, 2)
    tstep = 512

    def sample(i, carry):
        at = pl.multiple_of(i * tstep, tstep)
        ids = cell[:, pl.ds(at, tstep)]
        hot = onehot(ids // span, cells).astype(bf16)
        picked = mm(turned_hi, hot) + mm(turned_lo, hot)
        chosen = rows_iota(span, tstep) == (ids % span)
        got = []
        for k in range(4):
            part = jnp.where(chosen, picked[k * span : (k + 1) * span], 0.0)
            got.append(jnp.sum(part, axis=0, keepdims=True))
        for k in range(3):
            tract[k : k + 1, pl.ds(at, tstep)] = (
                got[0] * normal[k : k + 1, pl.ds(at, tstep)] + got[1 + k]
            )
        return carry

    lax.fori_loop(0, points // tstep, sample, 0)

    def gather_load(i, total):
        at = pl.multiple_of(i * step, step)
        chosen = rows_iota(nblocks, step) == group_of(at)
        spread = [jnp.where(chosen, tract[k : k + 1, pl.ds(at, step)], 0.0) for k in range(3)]
        upper, lower = pieces(jnp.concatenate(spread, axis=0), 2)
        first, second = whi[:, pl.ds(at, step)], wlo[:, pl.ds(at, step)]
        return total + (mm_nt(upper, first) + (mm_nt(lower, first) + mm_nt(upper, second)))

    load = lax.fori_loop(
        0, points // step, gather_load, jnp.zeros((3 * nblocks, BLOCK), f32)
    )
    for k in range(3):
        lsend[:, :, k] = load[k * nblocks : (k + 1) * nblocks].reshape(
            n_side, n_slab, SUB, BLOCK
        )
    exchange(2, "side", lambda peer: lsend.at[peer], lrecv.at[side])
    lrecv[side] = lsend[side]
    ready("comp")
    arrived(2, "side", lambda peer: lrecv.at[peer])
    psend[...] = jnp.sum(lrecv[...], axis=0)
    exchange(3, "slab", lambda peer: psend.at[peer], precv.at[slab])
    precv[slab] = psend[slab]
    arrived(3, "slab", lambda peer: precv.at[peer])
    load = jnp.sum(precv[...], axis=0)
    disp = spb[...] + comp[...][None] * (load - stiffed[...])
    dbuf[side, slab] = disp
    exchange(4, "slab", lambda peer: dbuf.at[side, slab], dbuf.at[side, slab])
    for hi in range(SUB):
        out_disp[:, hi * 128 : (hi + 1) * 128] = dbuf[side, slab, :, hi, :]
    arrived(4, "slab", lambda peer: dbuf.at[side, peer])
    exchange(5, "side", lambda peer: dbuf.at[side], dbuf.at[side])
    arrived(5, "side", lambda peer: dbuf.at[peer])

    field = jnp.concatenate([dbuf[:, :, k].reshape(nblocks, BLOCK) for k in range(3)], axis=0)
    field_hi, field_lo = pieces(field, 2)

    def map_back(i, carry):
        at = pl.multiple_of(i * step, step)
        first, second = whi[:, pl.ds(at, step)], wlo[:, pl.ds(at, step)]
        mapped = mm(field_hi, first) + (mm(field_lo, first) + mm(field_hi, second))
        chosen = rows_iota(nblocks, step) == group_of(at)
        for k in range(3):
            part = jnp.where(chosen, mapped[k * nblocks : (k + 1) * nblocks], 0.0)
            image[k : k + 1, pl.ds(at, step)] = jnp.sum(part, axis=0, keepdims=True)
        return carry

    lax.fori_loop(0, points // step, map_back, 0)

    ready("iterate", "rprev", "iprev")
    gram = None
    for k in range(3):
        now = image[k : k + 1, :]
        resid = now - iterate[k : k + 1, :]
        vcols[k, 0:1, :] = resid - rprev[k : k + 1, :]
        vcols[k, 1 + hist : 2 + hist, :] = resid
        wcols[k, 0:1, :] = now - iprev[k : k + 1, :]
        parts = stacked_pieces(vcols[k], 3)
        term = mm_nt(parts, parts)
        gram = term if gram is None else gram + term
    gram = gram[0:8] + gram[8:16] + gram[16:24]
    gram = gram[:, 0:8] + gram[:, 8:16] + gram[:, 16:24]
    gbuf[side] = jnp.concatenate([gram, jnp.zeros((8, BLOCK - 8), f32)], axis=1)
    exchange(6, "side", lambda peer: gbuf.at[side], gbuf.at[side])
    arrived(6, "side", lambda peer: gbuf.at[peer])
    hbuf[slab] = jnp.sum(gbuf[...], axis=0)
    exchange(7, "slab", lambda peer: hbuf.at[slab], hbuf.at[slab])
    arrived(7, "slab", lambda peer: hbuf.at[peer])
    sums = jnp.sum(hbuf[...], axis=0)
    size = hist + 1

    matrix = [[sums[i : i + 1, j : j + 1] for j in range(size)] for i in range(size)]
    rhs = [-sums[i : i + 1, size : size + 1] for i in range(size)]
    for pivot in range(size):
        scale = 1.0 / matrix[pivot][pivot]
        row_vals = [v * scale for v in matrix[pivot]]
        value = rhs[pivot] * scale
        for i in range(size):
            if i != pivot:
                factor = matrix[i][pivot]
                matrix[i] = [matrix[i][j] - factor * row_vals[j] for j in range(size)]
                rhs[i] = rhs[i] - factor * value
        matrix[pivot], rhs[pivot] = row_vals, value
    coeffs = jnp.concatenate(rhs + [jnp.zeros((8 - size, 1), f32)], axis=0)
    for k in range(3):
        change = jnp.sum(wcols[k] * coeffs, axis=0, keepdims=True)
        out_iter[k : k + 1, :] = image[k : k + 1, :] + change

    for copy in halo_copies:
        copy.wait_send()
    leaving.wait()
    departed(0, "slab", lambda peer: nbuf.at[side, slab])
    departed(1, "side", lambda peer: nbuf.at[side])
    departed(2, "side", lambda peer: lsend.at[peer])
    departed(3, "slab", lambda peer: psend.at[peer])
    departed(4, "slab", lambda peer: dbuf.at[side, slab])
    departed(5, "side", lambda peer: dbuf.at[side])
    departed(6, "side", lambda peer: gbuf.at[side])
    departed(7, "slab", lambda peer: hbuf.at[slab])


def body(n_slab, n_side, *args):
    (
        populations,
        solid_mask,
        point_cell,
        point_owner,
        point_block,
        point_coords,
        point_normal,
        node_coords,
        struct_prev,
        compliance,
        elem_nodes,
        elem_stiff,
        iterate,
        resid_prev,
        image_prev,
        resid_history,
        image_history,
    ) = args
    n = n_slab * n_side
    directions, depth, width, span = populations.shape
    points = point_cell.shape[0]
    elems = elem_nodes.shape[1]
    nblocks = n * SUB
    vmem = pl.BlockSpec(memory_space=pltpu.VMEM)
    DMA = pltpu.SemaphoreType.DMA
    operands = (
        populations,
        solid_mask,
        point_cell.reshape(1, points),
        point_owner.reshape(1, points),
        point_block.reshape(1, points),
        point_coords,
        point_normal,
        node_coords,
        struct_prev,
        compliance.reshape(SUB, BLOCK),
        elem_nodes,
        elem_stiff,
        iterate,
        resid_prev,
        image_prev,
        resid_history.transpose(1, 0, 2),
        image_history.transpose(1, 0, 2),
    )
    return pl.pallas_call(
        functools.partial(kernel, n_slab, n_side),
        out_shape=(
            jax.ShapeDtypeStruct(populations.shape, f32),
            jax.ShapeDtypeStruct(struct_prev.shape, f32),
            jax.ShapeDtypeStruct(iterate.shape, f32),
        ),
        in_specs=[pl.BlockSpec(memory_space=pltpu.HBM)] * len(operands),
        out_specs=(pl.BlockSpec(memory_space=pltpu.HBM), vmem, vmem),
        scratch_shapes=[
            pltpu.VMEM((directions, depth + 2, width + 2 * PAD, span), f32),
            pltpu.VMEM((4, depth * width, span), f32),
            pltpu.VMEM((2, 5, width, span), f32),
            pltpu.VMEM((2, 5, width, span), f32),
            pltpu.VMEM((2, 5, depth, span), f32),
            pltpu.VMEM((2, 5, depth, span), f32),
            pltpu.VMEM((4, 8, span), f32),
            pltpu.VMEM((4, 8, span), f32),
            pltpu.VMEM((n_side, n_slab, 3, SUB, BLOCK), f32),
            pltpu.VMEM((n_side, n_slab, 3, SUB, BLOCK), f32),
            pltpu.VMEM((n_side, n_slab, 3, SUB, BLOCK), f32),
            pltpu.VMEM((n_side, n_slab, 3, SUB, BLOCK), f32),
            pltpu.VMEM((n_side, 8, BLOCK), f32),
            pltpu.VMEM((3 * BLOCK, 3 * nblocks), bf16),
            pltpu.VMEM((3, SUB, BLOCK), f32),
            pltpu.VMEM((12, elems), f32),
            pltpu.VMEM((12, elems), f32),
            pltpu.VMEM((3, SUB, BLOCK), f32),
            pltpu.VMEM((BLOCK, points), bf16),
            pltpu.VMEM((BLOCK, points), bf16),
            pltpu.VMEM((3, points), f32),
            pltpu.VMEM((3, points), f32),
            DMA((8, max(n_slab, n_side))),
            DMA((8, max(n_slab, n_side))),
            DMA((HALO_SLOTS,)),
            DMA((HALO_SLOTS,)),
            pltpu.VMEM((3, 8, points), f32),
            pltpu.VMEM((3, 8, points), f32),
            DMA((len(operands),)),
            pltpu.VMEM((1, points), jnp.int32),
            pltpu.VMEM((n_slab, 3, SUB, BLOCK), f32),
            pltpu.VMEM((n_slab, 3, SUB, BLOCK), f32),
            pltpu.VMEM((n_slab, 8, BLOCK), f32),
            pltpu.VMEM(populations.shape, f32),
            DMA,
        ]
        + [pltpu.VMEM(x.shape, x.dtype) for x in operands],
        compiler_params=pltpu.CompilerParams(
            collective_id=0, has_side_effects=True, vmem_limit_bytes=63 * 2**20
        ),
    )(*operands)


def solution(mesh):
    lattice = P(None, ("groups", "slab"), "side", None)
    last = P(None, ("groups", "slab", "side"))
    one = P(("groups", "slab", "side"))
    deep = P(None, None, ("groups", "slab", "side"))
    return jax.shard_map(
        functools.partial(body, mesh.shape["slab"], mesh.shape["side"]),
        mesh=mesh,
        in_specs=(
            P(None, ("groups", "slab"), "side", None),
            P(("groups", "slab"), "side", None),
            one,
            P(("groups", "slab", "side"), None),
            one,
            last,
            last,
            last,
            last,
            one,
            last,
            deep,
            last,
            last,
            last,
            deep,
            deep,
        ),
        out_specs=(lattice, last, last),
        check_vma=False,
    )
```
